32 devices in a mesh: groups: 2 (over y), dp: 8 (over z, x), tensor: 2 (over core).
Axes of the slice: x: 2, y: 2, z: 4, core: 2. Of those that a mesh axis runs over, the one named last changes fastest.
Arguments:
- activations: bfloat16 [96, 48, 4096], P(('groups', 'dp'), None, 'tensor'), parts along dimension 0, may hold values from -6 to 6
- out_grads: bfloat16 [96, 48, 4096], P(('groups', 'dp'), None, 'tensor'), parts along dimension 0, may hold values from -6 to 6
- proj_in: bfloat16 [4096, 64], P('tensor'), may hold values from -0.09375 to 0.09375
- proj_out: bfloat16 [4096, 64], P('tensor'), may hold values from -0.09375 to 0.09375
- queries: bfloat16 [6144, 4096], P(('groups', 'dp', 'tensor')), parts along dimension 0, may hold values from -0.013671875 to 0.013671875
- domains: int32 [96, 2], P(('groups', 'dp')), parts along dimension 0, may hold values from 0 to 7, all different within a row; in each aligned block of 3 rows (0 to 2, 3 to 5, ...) at most 2 rows name the same one
Outputs:
- scores: float32 [96, 2, 384], P(('groups', 'dp', 'tensor')), parts along dimension 0
The draws below stay inside these ranges and needn't reach their ends.
There are 2 independent parts, one for each index of `groups`. The reference program is written for one: setup_inputs(seed, part) draws one part's arguments, and reference() takes and returns one part's arrays. A program takes and returns all parts, laid end to end along the dimension named above; an argument that names none is the same for every part. Nothing has to cross between parts.
Inputs may be any that keep to these rules, and one draw needn't show every extreme that they name: `domains`: each row names 2 different query blocks. In each aligned block of 3 rows no query block is named by more than 2 rows, and some query block is named by exactly 2 rows. The 6 rows of one index of dp span several aligned blocks, so they may name one query block more than 2 times: up to 2 in each aligned block.
All inputs are finite; a program needn't handle non-finite values.
Results may differ from the reference program's by a relative error of at most 0.0029.
Values may be sent and summed in bfloat16 or wider, within the bound.
No kernel may reach another device: no remote copies, remote signals or barrier semaphores. Data moves between devices by JAX's collectives and lax.ppermute only.
A program may use at most 64 MiB of HBM per device.

```python
import math
import jax
import jax.numpy as jnp
import numpy as np
from jax import lax

D = 4096
PROJ = 64
LEN = 48
CAP = 2
F = 4096
SEQ_SHARE = 3
K = 2
QB = 384
SEQS = 48
NQ = 3072
N_DP = 8


def level_of(rng, shape, shards, smallest, largest):
    level, own = 1.0, jax.random.fold_in(rng, 6)
    for axis_at, blocks in shards:
        steps = jnp.exp(jax.random.uniform(jax.random.fold_in(own, axis_at), (blocks,), jnp.float32, smallest / len(shards), largest / len(shards)))
        level = level * jnp.repeat(steps, shape[axis_at] // blocks).reshape([-1 if axis == axis_at else 1 for axis in range(len(shape))])
    return level


def deal_out(key, own, number, rows, count, top, bound, lean):
    sequence = jax.random.permutation(key, count)
    crowded, common = shares(count, rows * top, bound, lean, True), shares(count, rows * top, bound, lean, False)
    places = jnp.arange(count)

    def named(tallies, turn):
        used = int((tallies > 0).sum())
        fixed = max(1, used // 4)
        moved = fixed + (places - fixed + turn * (used - fixed)) % max(1, count - fixed)
        return jnp.zeros((count,), jnp.int32).at[sequence[jnp.where(places < fixed, places, moved)]].set(jnp.asarray(tallies, jnp.int32))

    tallies = jnp.where(number % 4 == 0, named(crowded, number // 4), named(common, number - number // 4 - 1))
    mixed = jax.random.permutation(jax.random.fold_in(own, 3), count)
    giver, taker = mixed[0:count // 2 * 2:2], mixed[1:count // 2 * 2:2]
    margin = jnp.minimum(tallies[giver] - 1, bound - tallies[taker]) // 2
    margin = jnp.where((giver == sequence[0]) | (taker == sequence[0]) | (tallies[taker] == 0), 0, jnp.maximum(margin, 0))
    moved = jax.random.randint(jax.random.fold_in(own, 4), (count // 2,), 0, 1 << 20) % (margin + 1)
    tallies = tallies.at[giver].add(-moved).at[taker].add(moved)
    members = jnp.searchsorted(jnp.cumsum(tallies), jnp.arange(rows * top), side="right").astype(jnp.int32)
    table = members.reshape(top, rows).T
    table = table[jax.random.permutation(jax.random.fold_in(own, 1), rows)]
    turn = jax.random.randint(jax.random.fold_in(own, 2), (rows, 1), 0, top)
    return jnp.take_along_axis(table, (jnp.arange(top)[None, :] + turn) % top, axis=1)


def shares(number_of, total, reach, skew, full):
    portions = [(1 << 20) // math.isqrt(grade ** skew) + 1 for grade in range(1, number_of + 1)]
    largest = reach if full else min(reach, max(-(-total // number_of), total * portions[0] // sum(portions)))
    least = 1 if total - largest >= number_of - 1 else 0
    counts, spare = [largest] + [least] * (number_of - 1), total - largest - least * (number_of - 1)
    while spare > 0:
        candidates = [i for i in range(1, number_of) if counts[i] < largest] or [i for i in range(1, number_of) if counts[i] < reach]
        mass, left = sum([portions[i] for i in candidates]), spare
        for i in candidates:
            addition = min(reach - counts[i], max(1, left * portions[i] // mass), spare)
            counts[i] = counts[i] + addition
            spare = spare - addition
    return np.array(counts)


def gaussian(stream_key, shape, width, most, pieces=(), dtype=jnp.bfloat16):
    level = level_of(stream_key, shape, pieces, -0.22, 0.18) if pieces else 1.0
    drawn = jax.random.normal(stream_key, shape, jnp.float32) * width * level
    return jnp.minimum(jnp.maximum(drawn, -most), most).astype(dtype)


def setup_inputs(seed: int = 0, part: int = 0) -> dict:
    keys = jax.random.split(jax.random.key(seed), 7)
    own_keys = jax.random.split(jax.random.fold_in(keys[6], part), 7)
    activations = gaussian(own_keys[0], (SEQS, LEN, D), 1.0, 6.0, ((0, 8), (2, 2)))
    out_grads = gaussian(own_keys[1], (SEQS, LEN, D), 1.0, 6.0, ((0, 8), (2, 2)))
    proj_in = gaussian(keys[2], (D, PROJ), D ** -0.5, 0.09375, ((0, 2),))
    proj_out = gaussian(keys[3], (D, PROJ), D ** -0.5, 0.09375, ((0, 2),))
    queries = gaussian(own_keys[4], (NQ, F), (F * LEN) ** -0.5, 0.013671875, ((0, 16),))
    domains_keys = jax.random.split(jax.random.fold_in(own_keys[5], 1), SEQS // SEQ_SHARE)
    domains_turns = jax.random.permutation(jax.random.fold_in(own_keys[5], 3), SEQS // SEQ_SHARE)
    domains = jax.vmap(lambda own, number: deal_out(jax.random.fold_in(own_keys[5], 2), own, number, SEQ_SHARE, N_DP, K, CAP, 2))(domains_keys, domains_turns).reshape((SEQS, K))
    return dict(activations=activations, out_grads=out_grads, proj_in=proj_in, proj_out=proj_out, queries=queries, domains=domains)


def reference(activations, out_grads, proj_in, proj_out, queries, domains):
    seq_count, length, in_width = activations.shape
    proj_acts = jnp.dot(activations.reshape(seq_count * length, in_width), proj_in, preferred_element_type=jnp.float32).reshape(seq_count, length, -1)
    proj_grads = jnp.dot(out_grads.reshape(seq_count * length, in_width), proj_out, preferred_element_type=jnp.float32).reshape(seq_count, length, -1)
    grams = jnp.einsum("stp,stq->spq", proj_grads, proj_acts, precision=lax.Precision.HIGHEST)
    features = grams.reshape(seq_count, -1).astype(jnp.bfloat16)
    feat_width = features.shape[1]
    blocks = queries.reshape(N_DP, QB, feat_width)

    def score_one(request_pair):
        feature, chosen = request_pair
        picked = blocks[chosen].reshape(-1, feat_width)
        return jnp.dot(picked, feature, preferred_element_type=jnp.float32).reshape(chosen.shape[0], QB)

    return lax.map(score_one, (features, domains))
```

```python
import functools

import jax
import jax.numpy as jnp
from jax import lax
from jax.experimental import pallas as pl
from jax.experimental.pallas import tpu as pltpu
from jax.sharding import PartitionSpec as P

CAP = 2
CHUNKS = 4
LANES = 128

VMEM = pl.BlockSpec(memory_space=pltpu.VMEM)
SMEM = pl.BlockSpec(memory_space=pltpu.SMEM)
ANY = pl.BlockSpec(memory_space=pl.ANY)


def each(count, step):
    if count <= 8:
        for at in range(count):
            step(at)
    else:
        lax.fori_loop(0, count, lambda at, _: (step(at), 0)[1], 0)


def project_kernel(acts, grads, p_in, p_out, out, acts_v, grads_v, in_v, out_v, sems):
    width = acts.shape[1]
    size = width // CHUNKS
    copies = []
    for side, (x, x_v, w, w_v) in enumerate(((acts, acts_v, p_in, in_v), (grads, grads_v, p_out, out_v))):
        for c in range(CHUNKS):
            part = pl.ds(c * size, size)
            copies.append(
                (
                    pltpu.make_async_copy(w.at[part], w_v.at[part], sems.at[side, c, 0]),
                    pltpu.make_async_copy(x.at[:, part], x_v.at[c], sems.at[side, c, 1]),
                )
            )
    for pair in copies:
        for copy in pair:
            copy.start()
    sums = []
    for side, (x_v, w_v) in enumerate(((acts_v, in_v), (grads_v, out_v))):
        total = None
        for c in range(CHUNKS):
            for copy in copies[side * CHUNKS + c]:
                copy.wait()
            term = jnp.dot(x_v[c], w_v[pl.ds(c * size, size)], preferred_element_type=jnp.float32)
            total = term if total is None else total + term
        sums.append(total)
    out[...] = jnp.concatenate(sums, axis=1)


def project(acts, grads, p_in, p_out):
    rows, width = acts.shape
    proj = p_in.shape[1]
    return pl.pallas_call(
        project_kernel,
        out_shape=jax.ShapeDtypeStruct((rows, 2 * proj), jnp.float32),
        in_specs=[ANY] * 4,
        out_specs=VMEM,
        scratch_shapes=[
            pltpu.VMEM((CHUNKS, rows, width // CHUNKS), jnp.bfloat16),
            pltpu.VMEM((CHUNKS, rows, width // CHUNKS), jnp.bfloat16),
            pltpu.VMEM((width, proj), jnp.bfloat16),
            pltpu.VMEM((width, proj), jnp.bfloat16),
            pltpu.SemaphoreType.DMA((2, CHUNKS, 2)),
        ],
        name="project",
    )(acts, grads, p_in, p_out)


def rank(domains, row, first, named):
    fanout = domains.shape[1]
    found = jnp.int32(0)
    for other in range(first, row):
        if fanout <= 8:
            for k in range(fanout):
                found += (domains[other, k] == named).astype(jnp.int32)
        else:
            found = lax.fori_loop(
                0, fanout, lambda k, n, other=other: n + (domains[other, k] == named).astype(jnp.int32), found
            )
    return found


def feature_kernel(share, domains, own, other, out, grams):
    seqs, fanout = domains.shape
    length = own.shape[0] // seqs
    proj = own.shape[1] // 2
    half = out.shape[2]
    out[...] = jnp.zeros_like(out)
    both = own[...] + other[...]
    high = both.astype(jnp.bfloat16)
    low = (both - high.astype(jnp.float32)).astype(jnp.bfloat16)
    mine = proj + lax.axis_index("tensor") * 2 * half
    left = lax.broadcasted_iota(jnp.int32, (half, LANES), 1) < proj
    for s in range(seqs):
        at = slice(s * length, (s + 1) * length)
        h, l = high[at], low[at]
        grams[s] = lax.dot_general(
            jnp.concatenate([h, l, h], axis=0),
            jnp.concatenate([h, h, l], axis=0),
            (((0,), (0,)), ((), ())),
            preferred_element_type=jnp.float32,
        )
    for s in range(seqs):
        even = grams[s, pl.ds(mine, half, stride=2), :]
        odd = grams[s, pl.ds(mine + 1, half, stride=2), :]
        feature = jnp.where(left, even, pltpu.roll(odd, proj, 1)).astype(out.dtype)
        group = s // share

        def place(k, s=s, group=group, feature=feature):
            named = domains[s, k]
            out[named, group * CAP + rank(domains, s, group * share, named)] = feature

        each(fanout, place)


def spread(domains, own, other, share, peers, tensor_count):
    seqs = domains.shape[0]
    proj = own.shape[1] // 2
    half = proj * proj // LANES // tensor_count
    return pl.pallas_call(
        functools.partial(feature_kernel, share),
        out_shape=jax.ShapeDtypeStruct((peers, seqs // share * CAP, half, LANES), jnp.bfloat16),
        in_specs=[SMEM, VMEM, VMEM],
        out_specs=VMEM,
        scratch_shapes=[pltpu.VMEM((seqs, 2 * proj, 2 * proj), jnp.float32)],
        name="spread",
    )(domains, own, other)


def score_kernel(features, own, other, out, rows_v):
    peers, slots, half, _ = features.shape
    count = peers * slots
    rows_v[...] = features[...].reshape(count * half, LANES).astype(jnp.float32)
    rows = jnp.concatenate(
        [rows_v[pl.ds(c, count, stride=half), :].astype(jnp.bfloat16) for c in range(half)], axis=1
    )
    me = lax.axis_index("tensor")
    part = pl.ds(pl.multiple_of(me * half * LANES, LANES), half * LANES)
    mine, theirs = (
        lax.dot_general(rows, q[:, part], (((1,), (1,)), ((), ())), preferred_element_type=jnp.float32)
        for q in (own, other)
    )
    scores = jnp.concatenate([jnp.where(me == 0, mine, theirs), jnp.where(me == 0, theirs, mine)], axis=1)
    for p in range(out.shape[0]):
        out[p] = scores[p * CAP : (p + 1) * CAP]


def score(features, own, other):
    peers, slots, half, _ = features.shape
    return pl.pallas_call(
        score_kernel,
        out_shape=jax.ShapeDtypeStruct((peers * slots // CAP, CAP, 2 * own.shape[0]), jnp.float32),
        in_specs=[VMEM] * 3,
        out_specs=VMEM,
        scratch_shapes=[pltpu.VMEM((peers * slots * half, LANES), jnp.float32)],
        name="score",
    )(features, own, other)


def pick_kernel(domains, scores, out):
    share, fanout, _ = out.shape
    first = lax.axis_index("tensor") * share
    for s in range(share):

        def take(k, s=s):
            named = domains[first + s, k]
            found = jnp.int32(0)
            for other in range(s):
                found += sum((domains[first + other, j] == named).astype(jnp.int32) for j in range(fanout))
            both = scores[2 * named] + scores[2 * named + 1]
            out[s, pl.ds(k, 1)] = jnp.where(found == 0, both[0:1], both[1:2])

        each(fanout, take)


def pick(domains, scores, share):
    return pl.pallas_call(
        pick_kernel,
        out_shape=jax.ShapeDtypeStruct((share, domains.shape[1], scores.shape[2]), jnp.float32),
        in_specs=[SMEM, VMEM],
        out_specs=VMEM,
        name="pick",
    )(domains, scores)


def body(activations, out_grads, proj_in, proj_out, queries, domains):
    seqs, length, width = activations.shape
    peers = lax.axis_size("dp")
    tensor_count = lax.axis_size("tensor")
    share = seqs // tensor_count
    swap = [(i, i ^ 1) for i in range(tensor_count)]
    own = project(
        activations.reshape(seqs * length, width), out_grads.reshape(seqs * length, width), proj_in, proj_out
    )
    other = lax.ppermute(own, "tensor", swap)
    other_queries = lax.ppermute(queries, "tensor", swap)
    sent = spread(domains, own, other, share, peers, tensor_count)
    came = lax.all_to_all(sent, "dp", split_axis=0, concat_axis=0, tiled=True)
    scores = score(came, queries, other_queries)
    back = lax.all_to_all(scores, ("dp", "tensor"), split_axis=0, concat_axis=0, tiled=True)
    return pick(domains, back, share)


def solution(mesh):
    placed = (
        P(("groups", "dp"), None, "tensor"),
        P(("groups", "dp"), None, "tensor"),
        P("tensor", None),
        P("tensor", None),
        P(("groups", "dp", "tensor"), None),
        P(("groups", "dp"), None),
    )
    return jax.shard_map(
        body,
        mesh=mesh,
        in_specs=placed,
        out_specs=P(("groups", "dp", "tensor"), None, None),
        check_vma=False,
    )
```

```python
import functools
import math

import jax
import jax.numpy as jnp
from jax import lax
from jax.experimental import pallas as pl
from jax.experimental.pallas import tpu as pltpu
from jax.sharding import PartitionSpec as P

CAP = 2
CHUNKS = 4
LANES = 128
LAST = (((1,), (1,)), ((), ()))

VMEM = pl.BlockSpec(memory_space=pltpu.VMEM)
SMEM = pl.BlockSpec(memory_space=pltpu.SMEM)
ANY = pl.BlockSpec(memory_space=pl.ANY)


def each(count, step):
    if count <= 8:
        for at in range(count):
            step(at)
    else:
        lax.fori_loop(0, count, lambda at, _: (step(at), 0)[1], 0)


def room(*shapes):
    held = sum(math.prod(shape) * jnp.dtype(dtype).itemsize for shape, dtype in shapes)
    return pltpu.CompilerParams(vmem_limit_bytes=2 * held + (1 << 20))


def project_kernel(acts, grads, p_in, p_out, out, acts_v, grads_v, in_v, out_v, sems):
    width = acts.shape[1]
    size = width // CHUNKS
    copies = []
    for side, (x, x_v, w, w_v) in enumerate(((acts, acts_v, p_in, in_v), (grads, grads_v, p_out, out_v))):
        for c in range(CHUNKS):
            part = pl.ds(c * size, size)
            copies.append(
                (
                    pltpu.make_async_copy(w.at[:, part], w_v.at[:, part], sems.at[side, c, 0]),
                    pltpu.make_async_copy(x.at[:, part], x_v.at[c], sems.at[side, c, 1]),
                )
            )
    for pair in copies:
        for copy in pair:
            copy.start()
    sums = []
    for side, (x_v, w_v) in enumerate(((acts_v, in_v), (grads_v, out_v))):
        total = None
        for c in range(CHUNKS):
            for copy in copies[side * CHUNKS + c]:
                copy.wait()
            term = lax.dot_general(x_v[c], w_v[:, pl.ds(c * size, size)], LAST, preferred_element_type=jnp.float32)
            total = term if total is None else total + term
        sums.append(total)
    out[...] = jnp.concatenate(sums, axis=1)


def project(acts, grads, p_in, p_out):
    rows, width = acts.shape
    proj = p_in.shape[0]
    bf16 = jnp.bfloat16
    return pl.pallas_call(
        project_kernel,
        out_shape=jax.ShapeDtypeStruct((rows, 2 * proj), jnp.float32),
        in_specs=[ANY] * 4,
        out_specs=VMEM,
        scratch_shapes=[
            pltpu.VMEM((CHUNKS, rows, width // CHUNKS), jnp.bfloat16),
            pltpu.VMEM((CHUNKS, rows, width // CHUNKS), jnp.bfloat16),
            pltpu.VMEM((proj, width), jnp.bfloat16),
            pltpu.VMEM((proj, width), jnp.bfloat16),
            pltpu.SemaphoreType.DMA((2, CHUNKS, 2)),
        ],
        compiler_params=room((acts.shape, bf16), (p_in.shape, bf16), ((rows, 2 * LANES), jnp.float32)),
        name="project",
    )(acts, grads, p_in, p_out)


def rank(domains, row, first, named):
    fanout = domains.shape[0]
    found = jnp.int32(0)
    for other in range(first, row):
        if fanout <= 8:
            for k in range(fanout):
                found += (domains[k, other] == named).astype(jnp.int32)
        else:
            found = lax.fori_loop(
                0, fanout, lambda k, n, other=other: n + (domains[k, other] == named).astype(jnp.int32), found
            )
    return found


def feature_kernel(share, domains, own, other, out, grams):
    fanout, seqs = domains.shape
    length = own.shape[0] // seqs
    proj = own.shape[1] // 2
    half = out.shape[2]
    out[...] = jnp.zeros_like(out)
    both = own[...] + other[...]
    high = both.astype(jnp.bfloat16)
    low = (both - high.astype(jnp.float32)).astype(jnp.bfloat16)
    mine = proj + lax.axis_index("tensor") * 2 * half
    left = lax.broadcasted_iota(jnp.int32, (half, LANES), 1) < proj
    for s in range(seqs):
        at = slice(s * length, (s + 1) * length)
        h, l = high[at], low[at]
        grams[s] = lax.dot_general(
            jnp.concatenate([h, l, h], axis=0),
            jnp.concatenate([h, h, l], axis=0),
            (((0,), (0,)), ((), ())),
            preferred_element_type=jnp.float32,
        )
    for s in range(seqs):
        even = grams[s, pl.ds(mine, half, stride=2), :]
        odd = grams[s, pl.ds(mine + 1, half, stride=2), :]
        feature = jnp.where(left, even, pltpu.roll(odd, proj, 1)).astype(out.dtype)
        group = s // share

        def place(k, s=s, group=group, feature=feature):
            named = domains[k, s]
            out[named, group * CAP + rank(domains, s, group * share, named)] = feature

        each(fanout, place)


def spread(domains, own, other, share, peers, tensor_count):
    seqs = domains.shape[1]
    proj = own.shape[1] // 2
    half = proj * proj // LANES // tensor_count
    return pl.pallas_call(
        functools.partial(feature_kernel, share),
        out_shape=jax.ShapeDtypeStruct((peers, seqs // share * CAP, half, LANES), jnp.bfloat16),
        in_specs=[SMEM, VMEM, VMEM],
        out_specs=VMEM,
        scratch_shapes=[pltpu.VMEM((seqs, 2 * proj, 2 * proj), jnp.float32)],
        compiler_params=room(
            ((4 * own.shape[0], LANES), jnp.float32), ((peers, seqs // share * CAP, half, LANES), jnp.bfloat16)
        ),
        name="spread",
    )(domains, own, other)


def score_kernel(features, own, other, out, rows_v):
    peers, slots, half, _ = features.shape
    count = peers * slots
    rows_v[...] = features[...].reshape(count * half, LANES).astype(jnp.float32)
    rows = jnp.concatenate(
        [rows_v[pl.ds(c, count, stride=half), :].astype(jnp.bfloat16) for c in range(half)], axis=1
    )
    me = lax.axis_index("tensor")
    part = pl.ds(pl.multiple_of(me * half * LANES, LANES), half * LANES)
    mine, theirs = (
        lax.dot_general(rows, q[:, part], LAST, preferred_element_type=jnp.float32)
        for q in (own, other)
    )
    scores = jnp.concatenate([jnp.where(me == 0, mine, theirs), jnp.where(me == 0, theirs, mine)], axis=1)
    for p in range(out.shape[0]):
        out[p] = scores[p * CAP : (p + 1) * CAP]


def score(features, own, other):
    peers, slots, half, _ = features.shape
    return pl.pallas_call(
        score_kernel,
        out_shape=jax.ShapeDtypeStruct((peers * slots // CAP, CAP, 2 * own.shape[0]), jnp.float32),
        in_specs=[VMEM] * 3,
        out_specs=VMEM,
        scratch_shapes=[pltpu.VMEM((peers * slots * half, LANES), jnp.float32)],
        compiler_params=room(
            (features.shape, jnp.bfloat16),
            ((peers * slots * half, LANES), jnp.float32),
            ((2 * own.shape[0], own.shape[1]), jnp.bfloat16),
            ((peers * slots // CAP, 8, 2 * own.shape[0]), jnp.float32),
        ),
        name="score",
    )(features, own, other)


def pick_kernel(domains, scores, out):
    share, fanout, _ = out.shape
    first = lax.axis_index("tensor") * share
    for s in range(share):

        def take(k, s=s):
            named = domains[k, first + s]
            found = jnp.int32(0)
            for other in range(s):
                found += sum((domains[j, first + other] == named).astype(jnp.int32) for j in range(fanout))
            both = scores[2 * named] + scores[2 * named + 1]
            out[s, pl.ds(k, 1)] = jnp.where(found == 0, both[0:1], both[1:2])

        each(fanout, take)


def pick(domains, scores, share):
    return pl.pallas_call(
        pick_kernel,
        out_shape=jax.ShapeDtypeStruct((share, domains.shape[0], scores.shape[2]), jnp.float32),
        in_specs=[SMEM, VMEM],
        out_specs=VMEM,
        compiler_params=room((scores.shape, jnp.float32), ((8 * share, domains.shape[0], scores.shape[2]), jnp.float32)),
        name="pick",
    )(domains, scores)


def body(activations, out_grads, proj_in, proj_out, queries, domains):
    seqs, length, width = activations.shape
    peers = lax.axis_size("dp")
    tensor_count = lax.axis_size("tensor")
    share = seqs // tensor_count
    swap = [(i, i ^ 1) for i in range(tensor_count)]
    own = project(
        activations.reshape(seqs * length, width), out_grads.reshape(seqs * length, width), proj_in.T, proj_out.T
    )
    domains = domains.T
    other = lax.ppermute(own, "tensor", swap)
    other_queries = lax.ppermute(queries, "tensor", swap)
    sent = spread(domains, own, other, share, peers, tensor_count)
    came = lax.all_to_all(sent, "dp", split_axis=0, concat_axis=0, tiled=True)
    scores = score(came, queries, other_queries)
    back = lax.all_to_all(scores, ("dp", "tensor"), split_axis=0, concat_axis=0, tiled=True)
    return pick(domains, back, share)


def solution(mesh):
    placed = (
        P(("groups", "dp"), None, "tensor"),
        P(("groups", "dp"), None, "tensor"),
        P("tensor", None),
        P("tensor", None),
        P(("groups", "dp", "tensor"), None),
        P(("groups", "dp"), None),
    )
    return jax.shard_map(
        body,
        mesh=mesh,
        in_specs=placed,
        out_specs=P(("groups", "dp", "tensor"), None, None),
        check_vma=False,
    )
```

```python
import functools
import math

import jax
import jax.numpy as jnp
from jax import lax
from jax.experimental import pallas as pl
from jax.experimental.pallas import tpu as pltpu
from jax.sharding import PartitionSpec as P

CAP = 2
CHUNKS = 4
LANES = 128
LAST = (((1,), (1,)), ((), ()))

VMEM = pl.BlockSpec(memory_space=pltpu.VMEM)
SMEM = pl.BlockSpec(memory_space=pltpu.SMEM)
ANY = pl.BlockSpec(memory_space=pl.ANY)


def each(count, step):
    if count <= 8:
        for at in range(count):
            step(at)
    else:
        lax.fori_loop(0, count, lambda at, _: (step(at), 0)[1], 0)


def near(*arrays):
    return [pltpu.with_memory_space_constraint(x, pltpu.VMEM) for x in arrays]


def far(*arrays):
    return [pltpu.with_memory_space_constraint(x, pltpu.HBM) for x in arrays]


def room(*shapes):
    held = sum(math.prod(shape) * jnp.dtype(dtype).itemsize for shape, dtype in shapes)
    return pltpu.CompilerParams(vmem_limit_bytes=2 * held + (1 << 20))


def project_kernel(acts, grads, p_in, p_out, out, acts_v, grads_v, in_v, out_v, sems):
    width = acts.shape[1]
    size = width // CHUNKS
    copies = []
    for side, (x, x_v, w, w_v) in enumerate(((acts, acts_v, p_in, in_v), (grads, grads_v, p_out, out_v))):
        for c in range(CHUNKS):
            part = pl.ds(c * size, size)
            copies.append(
                (
                    pltpu.make_async_copy(w.at[:, part], w_v.at[:, part], sems.at[side, c, 0]),
                    pltpu.make_async_copy(x.at[:, part], x_v.at[c], sems.at[side, c, 1]),
                )
            )
    for pair in copies:
        for copy in pair:
            copy.start()
    sums = []
    for side, (x_v, w_v) in enumerate(((acts_v, in_v), (grads_v, out_v))):
        total = None
        for c in range(CHUNKS):
            for copy in copies[side * CHUNKS + c]:
                copy.wait()
            term = lax.dot_general(x_v[c], w_v[:, pl.ds(c * size, size)], LAST, preferred_element_type=jnp.float32)
            total = term if total is None else total + term
        sums.append(total)
    out[...] = jnp.concatenate(sums, axis=1)


def project(acts, grads, p_in, p_out):
    rows, width = acts.shape
    proj = p_in.shape[0]
    bf16 = jnp.bfloat16
    return pl.pallas_call(
        project_kernel,
        out_shape=jax.ShapeDtypeStruct((rows, 2 * proj), jnp.float32),
        in_specs=[ANY] * 4,
        out_specs=VMEM,
        scratch_shapes=[
            pltpu.VMEM((CHUNKS, rows, width // CHUNKS), jnp.bfloat16),
            pltpu.VMEM((CHUNKS, rows, width // CHUNKS), jnp.bfloat16),
            pltpu.VMEM((proj, width), jnp.bfloat16),
            pltpu.VMEM((proj, width), jnp.bfloat16),
            pltpu.SemaphoreType.DMA((2, CHUNKS, 2)),
        ],
        compiler_params=room((acts.shape, bf16), (p_in.shape, bf16), ((rows, 2 * LANES), jnp.float32)),
        name="project",
    )(*far(acts, grads, p_in, p_out))


def rank(domains, row, first, named):
    fanout = domains.shape[0]
    found = jnp.int32(0)
    for other in range(first, row):
        if fanout <= 8:
            for k in range(fanout):
                found += (domains[k, other] == named).astype(jnp.int32)
        else:
            found = lax.fori_loop(
                0, fanout, lambda k, n, other=other: n + (domains[k, other] == named).astype(jnp.int32), found
            )
    return found


def feature_kernel(share, domains, own, other, out, grams):
    fanout, seqs = domains.shape
    length = own.shape[0] // seqs
    proj = own.shape[1] // 2
    half = out.shape[2]
    out[...] = jnp.zeros_like(out)
    both = own[...] + other[...]
    high = both.astype(jnp.bfloat16)
    low = (both - high.astype(jnp.float32)).astype(jnp.bfloat16)
    mine = proj + lax.axis_index("tensor") * 2 * half
    left = lax.broadcasted_iota(jnp.int32, (half, LANES), 1) < proj
    for s in range(seqs):
        at = slice(s * length, (s + 1) * length)
        h, l = high[at], low[at]
        grams[s] = lax.dot_general(
            jnp.concatenate([h, l, h], axis=0),
            jnp.concatenate([h, h, l], axis=0),
            (((0,), (0,)), ((), ())),
            preferred_element_type=jnp.float32,
        )
    for s in range(seqs):
        even = grams[s, pl.ds(mine, half, stride=2), :]
        odd = grams[s, pl.ds(mine + 1, half, stride=2), :]
        feature = jnp.where(left, even, pltpu.roll(odd, proj, 1)).astype(out.dtype)
        group = s // share

        def place(k, s=s, group=group, feature=feature):
            named = domains[k, s]
            out[named, group * CAP + rank(domains, s, group * share, named)] = feature

        each(fanout, place)


def spread(domains, own, other, share, peers, tensor_count):
    seqs = domains.shape[1]
    proj = own.shape[1] // 2
    half = proj * proj // LANES // tensor_count
    return pl.pallas_call(
        functools.partial(feature_kernel, share),
        out_shape=jax.ShapeDtypeStruct((peers, seqs // share * CAP, half, LANES), jnp.bfloat16),
        in_specs=[SMEM, VMEM, VMEM],
        out_specs=VMEM,
        scratch_shapes=[pltpu.VMEM((seqs, 2 * proj, 2 * proj), jnp.float32)],
        compiler_params=room(
            ((4 * own.shape[0], LANES), jnp.float32), ((peers, seqs // share * CAP, half, LANES), jnp.bfloat16)
        ),
        name="spread",
    )(domains, *near(own, other))


def score_kernel(features, own, other, out, rows_v):
    peers, slots, half, _ = features.shape
    count = peers * slots
    rows_v[...] = features[...].reshape(count * half, LANES).astype(jnp.float32)
    rows = jnp.concatenate(
        [rows_v[pl.ds(c, count, stride=half), :].astype(jnp.bfloat16) for c in range(half)], axis=1
    )
    me = lax.axis_index("tensor")
    part = pl.ds(pl.multiple_of(me * half * LANES, LANES), half * LANES)
    mine, theirs = (
        lax.dot_general(rows, q[:, part], LAST, preferred_element_type=jnp.float32)
        for q in (own, other)
    )
    scores = jnp.concatenate([jnp.where(me == 0, mine, theirs), jnp.where(me == 0, theirs, mine)], axis=1)
    for p in range(out.shape[0]):
        out[p] = scores[p * CAP : (p + 1) * CAP]


def score(features, own, other):
    peers, slots, half, _ = features.shape
    return pl.pallas_call(
        score_kernel,
        out_shape=jax.ShapeDtypeStruct((peers * slots // CAP, CAP, 2 * own.shape[0]), jnp.float32),
        in_specs=[VMEM] * 3,
        out_specs=VMEM,
        scratch_shapes=[pltpu.VMEM((peers * slots * half, LANES), jnp.float32)],
        compiler_params=room(
            (features.shape, jnp.bfloat16),
            ((peers * slots * half, LANES), jnp.float32),
            ((2 * own.shape[0], own.shape[1]), jnp.bfloat16),
            ((peers * slots // CAP, 8, 2 * own.shape[0]), jnp.float32),
        ),
        name="score",
    )(*near(features, own, other))


def pick_kernel(domains, scores, out):
    share, fanout, _ = out.shape
    first = lax.axis_index("tensor") * share
    for s in range(share):

        def take(k, s=s):
            named = domains[k, first + s]
            found = jnp.int32(0)
            for other in range(s):
                found += sum((domains[j, first + other] == named).astype(jnp.int32) for j in range(fanout))
            both = scores[2 * named] + scores[2 * named + 1]
            out[s, pl.ds(k, 1)] = jnp.where(found == 0, both[0:1], both[1:2])

        each(fanout, take)


def pick(domains, scores, share):
    return pl.pallas_call(
        pick_kernel,
        out_shape=jax.ShapeDtypeStruct((share, domains.shape[0], scores.shape[2]), jnp.float32),
        in_specs=[SMEM, VMEM],
        out_specs=VMEM,
        compiler_params=room((scores.shape, jnp.float32), ((8 * share, domains.shape[0], scores.shape[2]), jnp.float32)),
        name="pick",
    )(domains, *near(scores))


def body(activations, out_grads, proj_in, proj_out, queries, domains):
    seqs, length, width = activations.shape
    peers = lax.axis_size("dp")
    tensor_count = lax.axis_size("tensor")
    share = seqs // tensor_count
    swap = [(i, i ^ 1) for i in range(tensor_count)]
    own = project(
        activations.reshape(seqs * length, width), out_grads.reshape(seqs * length, width), proj_in.T, proj_out.T
    )
    domains = domains.T
    other = lax.ppermute(own, "tensor", swap)
    other_queries = lax.ppermute(queries, "tensor", swap)
    sent = spread(domains, own, other, share, peers, tensor_count)
    came = lax.all_to_all(sent, "dp", split_axis=0, concat_axis=0, tiled=True)
    scores = score(came, queries, other_queries)
    back = lax.all_to_all(scores, ("dp", "tensor"), split_axis=0, concat_axis=0, tiled=True)
    return pick(domains, back, share)


def solution(mesh):
    placed = (
        P(("groups", "dp"), None, "tensor"),
        P(("groups", "dp"), None, "tensor"),
        P("tensor", None),
        P("tensor", None),
        P(("groups", "dp", "tensor"), None),
        P(("groups", "dp"), None),
    )
    return jax.shard_map(
        body,
        mesh=mesh,
        in_specs=placed,
        out_specs=P(("groups", "dp", "tensor"), None, None),
        check_vma=False,
    )
```

```python
import functools
import math

import jax
import jax.numpy as jnp
from jax import lax
from jax.experimental import pallas as pl
from jax.experimental.pallas import tpu as pltpu
from jax.sharding import PartitionSpec as P

CAP = 2
CHUNKS = 4
LANES = 128
LAST = (((1,), (1,)), ((), ()))

VMEM = pl.BlockSpec(memory_space=pltpu.VMEM)
SMEM = pl.BlockSpec(memory_space=pltpu.SMEM)
ANY = pl.BlockSpec(memory_space=pl.ANY)


def each(count, step):
    if count <= 8:
        for at in range(count):
            step(at)
    else:
        lax.fori_loop(0, count, lambda at, _: (step(at), 0)[1], 0)


def near(*arrays):
    return [pltpu.with_memory_space_constraint(x, pltpu.VMEM) for x in arrays]


def far(*arrays):
    return [pltpu.with_memory_space_constraint(x, pltpu.HBM) for x in arrays]


def room(*shapes):
    held = sum(math.prod(shape) * jnp.dtype(dtype).itemsize for shape, dtype in shapes)
    return pltpu.CompilerParams(vmem_limit_bytes=2 * held + (1 << 20))


def project_kernel(acts, grads, p_in, p_out, out, acts_v, grads_v, in_v, out_v, sems):
    width = acts.shape[1]
    size = width // CHUNKS
    copies = []
    for side, (x, x_v, w, w_v) in enumerate(((acts, acts_v, p_in, in_v), (grads, grads_v, p_out, out_v))):
        for c in range(CHUNKS):
            part = pl.ds(c * size, size)
            copies.append(
                (
                    pltpu.make_async_copy(w.at[:, part], w_v.at[:, part], sems.at[side, c, 0]),
                    pltpu.make_async_copy(x.at[:, part], x_v.at[c], sems.at[side, c, 1]),
                )
            )
    for pair in copies:
        for copy in pair:
            copy.start()
    sums = []
    for side, (x_v, w_v) in enumerate(((acts_v, in_v), (grads_v, out_v))):
        total = None
        for c in range(CHUNKS):
            for copy in copies[side * CHUNKS + c]:
                copy.wait()
            term = lax.dot_general(x_v[c], w_v[:, pl.ds(c * size, size)], LAST, preferred_element_type=jnp.float32)
            total = term if total is None else total + term
        sums.append(total)
    out[...] = jnp.concatenate(sums, axis=1)


def project(acts, grads, p_in, p_out):
    rows, width = acts.shape
    proj = p_in.shape[0]
    bf16 = jnp.bfloat16
    return pl.pallas_call(
        project_kernel,
        out_shape=jax.ShapeDtypeStruct((rows, 2 * proj), jnp.float32),
        in_specs=[ANY] * 4,
        out_specs=VMEM,
        scratch_shapes=[
            pltpu.VMEM((CHUNKS, rows, width // CHUNKS), jnp.bfloat16),
            pltpu.VMEM((CHUNKS, rows, width // CHUNKS), jnp.bfloat16),
            pltpu.VMEM((proj, width), jnp.bfloat16),
            pltpu.VMEM((proj, width), jnp.bfloat16),
            pltpu.SemaphoreType.DMA((2, CHUNKS, 2)),
        ],
        compiler_params=room((acts.shape, bf16), (p_in.shape, bf16), ((rows, 2 * LANES), jnp.float32)),
        name="project",
    )(*far(acts, grads, p_in, p_out))


def rank(domains, row, first, named):
    fanout = domains.shape[0]
    found = jnp.int32(0)
    for other in range(first, row):
        if fanout <= 8:
            for k in range(fanout):
                found += (domains[k, other] == named).astype(jnp.int32)
        else:
            found = lax.fori_loop(
                0, fanout, lambda k, n, other=other: n + (domains[k, other] == named).astype(jnp.int32), found
            )
    return found


def feature_kernel(share, domains_in, own, other, out, grams, domains, sem):
    fetch = pltpu.make_async_copy(domains_in, domains, sem)
    fetch.start()
    fanout, seqs = domains.shape
    length = own.shape[0] // seqs
    proj = own.shape[1] // 2
    half = out.shape[2]
    out[...] = jnp.zeros_like(out)
    both = own[...] + other[...]
    high = both.astype(jnp.bfloat16)
    low = (both - high.astype(jnp.float32)).astype(jnp.bfloat16)
    mine = proj + lax.axis_index("tensor") * 2 * half
    left = lax.broadcasted_iota(jnp.int32, (half, LANES), 1) < proj
    for s in range(seqs):
        at = slice(s * length, (s + 1) * length)
        h, l = high[at], low[at]
        grams[s] = lax.dot_general(
            jnp.concatenate([h, l, h], axis=0),
            jnp.concatenate([h, h, l], axis=0),
            (((0,), (0,)), ((), ())),
            preferred_element_type=jnp.float32,
        )
    fetch.wait()
    for s in range(seqs):
        even = grams[s, pl.ds(mine, half, stride=2), :]
        odd = grams[s, pl.ds(mine + 1, half, stride=2), :]
        feature = jnp.where(left, even, pltpu.roll(odd, proj, 1)).astype(out.dtype)
        group = s // share

        def place(k, s=s, group=group, feature=feature):
            named = domains[k, s]
            out[named, group * CAP + rank(domains, s, group * share, named)] = feature

        each(fanout, place)


def spread(domains, own, other, share, peers, tensor_count):
    seqs = domains.shape[1]
    proj = own.shape[1] // 2
    half = proj * proj // LANES // tensor_count
    return pl.pallas_call(
        functools.partial(feature_kernel, share),
        out_shape=jax.ShapeDtypeStruct((peers, seqs // share * CAP, half, LANES), jnp.bfloat16),
        in_specs=[ANY, VMEM, VMEM],
        out_specs=VMEM,
        scratch_shapes=[
            pltpu.VMEM((seqs, 2 * proj, 2 * proj), jnp.float32),
            pltpu.SMEM(domains.shape, jnp.int32),
            pltpu.SemaphoreType.DMA,
        ],
        compiler_params=room(
            ((4 * own.shape[0], LANES), jnp.float32), ((peers, seqs // share * CAP, half, LANES), jnp.bfloat16)
        ),
        name="spread",
    )(domains, *near(own, other))


def score_kernel(features, own, other, out, rows_v):
    peers, slots, half, _ = features.shape
    count = peers * slots
    rows_v[...] = features[...].reshape(count * half, LANES).astype(jnp.float32)
    rows = jnp.concatenate(
        [rows_v[pl.ds(c, count, stride=half), :].astype(jnp.bfloat16) for c in range(half)], axis=1
    )
    me = lax.axis_index("tensor")
    part = pl.ds(pl.multiple_of(me * half * LANES, LANES), half * LANES)
    mine, theirs = (
        lax.dot_general(rows, q[:, part], LAST, preferred_element_type=jnp.float32)
        for q in (own, other)
    )
    scores = jnp.concatenate([jnp.where(me == 0, mine, theirs), jnp.where(me == 0, theirs, mine)], axis=1)
    for p in range(out.shape[0]):
        out[p] = scores[p * CAP : (p + 1) * CAP]


def score(features, own, other):
    peers, slots, half, _ = features.shape
    return pl.pallas_call(
        score_kernel,
        out_shape=jax.ShapeDtypeStruct((peers * slots // CAP, CAP, 2 * own.shape[0]), jnp.float32),
        in_specs=[VMEM] * 3,
        out_specs=VMEM,
        scratch_shapes=[pltpu.VMEM((peers * slots * half, LANES), jnp.float32)],
        compiler_params=room(
            (features.shape, jnp.bfloat16),
            ((peers * slots * half, LANES), jnp.float32),
            ((2 * own.shape[0], own.shape[1]), jnp.bfloat16),
            ((peers * slots // CAP, 8, 2 * own.shape[0]), jnp.float32),
        ),
        name="score",
    )(*near(features, own, other))


def plan_kernel(share, domains, own, out):
    del own
    fanout = domains.shape[0]
    first = lax.axis_index("tensor") * share
    column = lax.broadcasted_iota(jnp.int32, (1, out.shape[1]), 1)
    out[...] = jnp.zeros_like(out)
    for s in range(share):

        def mark(k, s=s):
            named = domains[k, first + s]
            found = jnp.int32(0)
            for other in range(s):
                found += sum((domains[j, first + other] == named).astype(jnp.int32) for j in range(fanout))
            row = 2 * CAP * named + found
            out[pl.ds(s * fanout + k, 1)] = ((column == row) | (column == row + CAP)).astype(jnp.float32)

        each(fanout, mark)


def plan(domains, own, share, count):
    rows = -(-share * domains.shape[0] // 8) * 8
    return pl.pallas_call(
        functools.partial(plan_kernel, share),
        out_shape=jax.ShapeDtypeStruct((rows, count), jnp.float32),
        in_specs=[SMEM, ANY],
        out_specs=VMEM,
        compiler_params=room(((rows, max(count, LANES)), jnp.float32)),
        name="plan",
    )(domains, own)


def pick_kernel(chosen, scores, out):
    share, fanout, _ = out.shape
    rows = jnp.concatenate([scores[p] for p in range(scores.shape[0])], axis=0)
    picked = jnp.dot(chosen[...], rows, precision=lax.Precision.HIGHEST, preferred_element_type=jnp.float32)
    for s in range(share):
        out[s] = picked[s * fanout : (s + 1) * fanout]


def pick(chosen, scores, share, fanout):
    return pl.pallas_call(
        pick_kernel,
        out_shape=jax.ShapeDtypeStruct((share, fanout, scores.shape[2]), jnp.float32),
        in_specs=[VMEM, VMEM],
        out_specs=VMEM,
        compiler_params=room((scores.shape, jnp.float32), (scores.shape, jnp.float32), (chosen.shape, jnp.float32)),
        name="pick",
    )(*near(chosen, scores))


def body(activations, out_grads, proj_in, proj_out, queries, domains):
    seqs, length, width = activations.shape
    peers = lax.axis_size("dp")
    tensor_count = lax.axis_size("tensor")
    share = seqs // tensor_count
    swap = [(i, i ^ 1) for i in range(tensor_count)]
    own = project(
        activations.reshape(seqs * length, width), out_grads.reshape(seqs * length, width), proj_in.T, proj_out.T
    )
    domains = domains.T
    other = lax.ppermute(own, "tensor", swap)
    chosen = plan(domains, own, share, peers * tensor_count * CAP)
    queries, other, chosen = lax.optimization_barrier((queries, other, chosen))
    other_queries = lax.ppermute(queries, "tensor", swap)
    sent = spread(domains, own, other, share, peers, tensor_count)
    came = lax.all_to_all(sent, "dp", split_axis=0, concat_axis=0, tiled=True)
    scores = score(came, queries, other_queries)
    back = lax.all_to_all(scores, ("dp", "tensor"), split_axis=0, concat_axis=0, tiled=True)
    return pick(chosen, back, share, domains.shape[0])


def solution(mesh):
    placed = (
        P(("groups", "dp"), None, "tensor"),
        P(("groups", "dp"), None, "tensor"),
        P("tensor", None),
        P("tensor", None),
        P(("groups", "dp", "tensor"), None),
        P(("groups", "dp"), None),
    )
    return jax.shard_map(
        body,
        mesh=mesh,
        in_specs=placed,
        out_specs=P(("groups", "dp", "tensor"), None, None),
        check_vma=False,
    )
```

```python
import functools
import math

import jax
import jax.numpy as jnp
from jax import lax
from jax.experimental import pallas as pl
from jax.experimental.pallas import tpu as pltpu
from jax.sharding import PartitionSpec as P

CAP = 2
LANES = 128
LAST = (((1,), (1,)), ((), ()))

VMEM = pl.BlockSpec(memory_space=pltpu.VMEM)
SMEM = pl.BlockSpec(memory_space=pltpu.SMEM)
ANY = pl.BlockSpec(memory_space=pl.ANY)


def each(count, step):
    if count <= 8:
        for at in range(count):
            step(at)
    else:
        lax.fori_loop(0, count, lambda at, _: (step(at), 0)[1], 0)


def near(*arrays):
    return [pltpu.with_memory_space_constraint(x, pltpu.VMEM) for x in arrays]


def far(*arrays):
    return [pltpu.with_memory_space_constraint(x, pltpu.HBM) for x in arrays]


def room(*shapes):
    held = sum(math.prod(shape) * jnp.dtype(dtype).itemsize for shape, dtype in shapes)
    return pltpu.CompilerParams(vmem_limit_bytes=2 * held + (1 << 20))


def project_kernel(acts, grads, p_in, p_out, out, x_v, w_v, sums, sems):
    for side, (x, w) in enumerate(((acts, p_in), (grads, p_out))):
        pltpu.make_async_copy(w, w_v.at[side], sems.at[side, 0]).start()
        pltpu.make_async_copy(x, x_v.at[side], sems.at[side, 1]).start()

    @pl.loop(0, 2)
    def _(side):
        pltpu.make_async_copy(p_in, w_v.at[side], sems.at[side, 0]).wait()
        pltpu.make_async_copy(acts, x_v.at[side], sems.at[side, 1]).wait()
        sums[side] = lax.dot_general(x_v[side], w_v[side], LAST, preferred_element_type=jnp.float32)

    out[...] = jnp.concatenate([sums[0], sums[1]], axis=1)


def project(acts, grads, p_in, p_out):
    rows, width = acts.shape
    proj = p_in.shape[0]
    bf16 = jnp.bfloat16
    return pl.pallas_call(
        project_kernel,
        out_shape=jax.ShapeDtypeStruct((rows, 2 * proj), jnp.float32),
        in_specs=[ANY] * 4,
        out_specs=VMEM,
        scratch_shapes=[
            pltpu.VMEM((2, rows, width), bf16),
            pltpu.VMEM((2, proj, width), bf16),
            pltpu.VMEM((2, rows, proj), jnp.float32),
            pltpu.SemaphoreType.DMA((2, 2)),
        ],
        compiler_params=room((acts.shape, bf16), (p_in.shape, bf16), ((rows, 4 * LANES), jnp.float32)),
        name="project",
    )(*far(acts, grads, p_in, p_out))


def rank(domains, row, first, named):
    fanout = domains.shape[0]
    found = jnp.int32(0)
    for other in range(first, row):
        if fanout <= 8:
            for k in range(fanout):
                found += (domains[k, other] == named).astype(jnp.int32)
        else:
            found = lax.fori_loop(
                0, fanout, lambda k, n, other=other: n + (domains[k, other] == named).astype(jnp.int32), found
            )
    return found


def feature_kernel(share, domains_in, own, other, out, grams, domains, sem):
    fetch = pltpu.make_async_copy(domains_in, domains, sem)
    fetch.start()
    fanout, seqs = domains.shape
    length = own.shape[0] // seqs
    proj = own.shape[1] // 2
    half = out.shape[2]
    out[...] = jnp.zeros_like(out)
    both = own[...] + other[...]
    high = both.astype(jnp.bfloat16)
    low = (both - high.astype(jnp.float32)).astype(jnp.bfloat16)
    mine = proj + lax.axis_index("tensor") * 2 * half
    left = lax.broadcasted_iota(jnp.int32, (half, LANES), 1) < proj
    for s in range(seqs):
        at = slice(s * length, (s + 1) * length)
        h, l = high[at], low[at]
        grams[s] = lax.dot_general(
            jnp.concatenate([h, l, h], axis=0),
            jnp.concatenate([h, h, l], axis=0),
            (((0,), (0,)), ((), ())),
            preferred_element_type=jnp.float32,
        )
    fetch.wait()
    for s in range(seqs):
        even = grams[s, pl.ds(mine, half, stride=2), :]
        odd = grams[s, pl.ds(mine + 1, half, stride=2), :]
        feature = jnp.where(left, even, pltpu.roll(odd, proj, 1)).astype(out.dtype)
        group = s // share

        def place(k, s=s, group=group, feature=feature):
            named = domains[k, s]
            out[named, group * CAP + rank(domains, s, group * share, named)] = feature

        each(fanout, place)


def spread(domains, own, other, share, peers, tensor_count):
    seqs = domains.shape[1]
    proj = own.shape[1] // 2
    half = proj * proj // LANES // tensor_count
    return pl.pallas_call(
        functools.partial(feature_kernel, share),
        out_shape=jax.ShapeDtypeStruct((peers, seqs // share * CAP, half, LANES), jnp.bfloat16),
        in_specs=[ANY, VMEM, VMEM],
        out_specs=VMEM,
        scratch_shapes=[
            pltpu.VMEM((seqs, 2 * proj, 2 * proj), jnp.float32),
            pltpu.SMEM(domains.shape, jnp.int32),
            pltpu.SemaphoreType.DMA,
        ],
        compiler_params=room(
            ((4 * own.shape[0], LANES), jnp.float32), ((peers, seqs // share * CAP, half, LANES), jnp.bfloat16)
        ),
        cost_estimate=pl.CostEstimate(flops=50_000_000_000, bytes_accessed=1 << 20, transcendentals=0),
        name="spread",
    )(domains, *near(own, other))


def score_kernel(features, own, other, out, rows_v):
    peers, slots, half, _ = features.shape
    count = peers * slots
    rows_v[...] = features[...].reshape(count * half, LANES).astype(jnp.float32)
    rows = jnp.concatenate(
        [rows_v[pl.ds(c, count, stride=half), :].astype(jnp.bfloat16) for c in range(half)], axis=1
    )
    me = lax.axis_index("tensor")
    part = pl.ds(pl.multiple_of(me * half * LANES, LANES), half * LANES)
    mine, theirs = (
        lax.dot_general(rows, q[:, part], LAST, preferred_element_type=jnp.float32)
        for q in (own, other)
    )
    scores = jnp.concatenate([jnp.where(me == 0, mine, theirs), jnp.where(me == 0, theirs, mine)], axis=1)
    for p in range(out.shape[0]):
        out[p] = scores[p * CAP : (p + 1) * CAP]


def score(features, own, other):
    peers, slots, half, _ = features.shape
    return pl.pallas_call(
        score_kernel,
        out_shape=jax.ShapeDtypeStruct((peers * slots // CAP, CAP, 2 * own.shape[0]), jnp.float32),
        in_specs=[VMEM] * 3,
        out_specs=VMEM,
        scratch_shapes=[pltpu.VMEM((peers * slots * half, LANES), jnp.float32)],
        compiler_params=room(
            (features.shape, jnp.bfloat16),
            ((peers * slots * half, LANES), jnp.float32),
            ((2 * own.shape[0], own.shape[1]), jnp.bfloat16),
            ((peers * slots // CAP, 8, 2 * own.shape[0]), jnp.float32),
        ),
        name="score",
    )(*near(features, own, other))


def plan_kernel(share, domains, own, out):
    del own
    fanout = domains.shape[0]
    first = lax.axis_index("tensor") * share
    column = lax.broadcasted_iota(jnp.int32, (1, out.shape[1]), 1)
    out[...] = jnp.zeros_like(out)
    for s in range(share):

        def mark(k, s=s):
            named = domains[k, first + s]
            found = jnp.int32(0)
            for other in range(s):
                found += sum((domains[j, first + other] == named).astype(jnp.int32) for j in range(fanout))
            row = 2 * CAP * named + found
            out[pl.ds(s * fanout + k, 1)] = ((column == row) | (column == row + CAP)).astype(jnp.float32)

        each(fanout, mark)


def plan(domains, own, share, count):
    rows = -(-share * domains.shape[0] // 8) * 8
    return pl.pallas_call(
        functools.partial(plan_kernel, share),
        out_shape=jax.ShapeDtypeStruct((rows, count), jnp.float32),
        in_specs=[SMEM, ANY],
        out_specs=VMEM,
        compiler_params=room(((rows, max(count, LANES)), jnp.float32)),
        name="plan",
    )(domains, own)


def pick_kernel(chosen, scores, out):
    share, fanout, _ = out.shape
    rows = jnp.concatenate([scores[p] for p in range(scores.shape[0])], axis=0)
    picked = jnp.dot(chosen[...], rows, precision=lax.Precision.HIGHEST, preferred_element_type=jnp.float32)
    for s in range(share):
        out[s] = picked[s * fanout : (s + 1) * fanout]


def pick(chosen, scores, share, fanout):
    return pl.pallas_call(
        pick_kernel,
        out_shape=jax.ShapeDtypeStruct((share, fanout, scores.shape[2]), jnp.float32),
        in_specs=[VMEM, VMEM],
        out_specs=VMEM,
        compiler_params=room((scores.shape, jnp.float32), (scores.shape, jnp.float32), (chosen.shape, jnp.float32)),
        name="pick",
    )(*near(chosen, scores))


def body(activations, out_grads, proj_in, proj_out, queries, domains):
    seqs, length, width = activations.shape
    peers = lax.axis_size("dp")
    tensor_count = lax.axis_size("tensor")
    share = seqs // tensor_count
    swap = [(i, i ^ 1) for i in range(tensor_count)]
    own = project(
        activations.reshape(seqs * length, width), out_grads.reshape(seqs * length, width), proj_in.T, proj_out.T
    )
    domains = domains.T
    other = lax.ppermute(own, "tensor", swap)
    chosen = plan(domains, own, share, peers * tensor_count * CAP)
    queries, chosen = lax.optimization_barrier((queries, chosen))
    other_queries = lax.ppermute(queries, "tensor", swap)
    sent = spread(domains, own, other, share, peers, tensor_count)
    came = lax.all_to_all(sent, "dp", split_axis=0, concat_axis=0, tiled=True)
    scores = score(came, queries, other_queries)
    back = lax.all_to_all(scores, ("dp", "tensor"), split_axis=0, concat_axis=0, tiled=True)
    return pick(chosen, back, share, domains.shape[0])


def solution(mesh):
    placed = (
        P(("groups", "dp"), None, "tensor"),
        P(("groups", "dp"), None, "tensor"),
        P("tensor", None),
        P("tensor", None),
        P(("groups", "dp", "tensor"), None),
        P(("groups", "dp"), None),
    )
    return jax.shard_map(
        body,
        mesh=mesh,
        in_specs=placed,
        out_specs=P(("groups", "dp", "tensor"), None, None),
        check_vma=False,
    )
```

```python
import functools
import math

import jax
import jax.numpy as jnp
from jax import lax
from jax.experimental import pallas as pl
from jax.experimental.pallas import tpu as pltpu
from jax.sharding import PartitionSpec as P

CAP = 2
LANES = 128
LAST = (((1,), (1,)), ((), ()))

VMEM = pl.BlockSpec(memory_space=pltpu.VMEM)
SMEM = pl.BlockSpec(memory_space=pltpu.SMEM)
ANY = pl.BlockSpec(memory_space=pl.ANY)


def each(count, step):
    if count <= 8:
        for at in range(count):
            step(at)
    else:
        lax.fori_loop(0, count, lambda at, _: (step(at), 0)[1], 0)


def near(*arrays):
    return [pltpu.with_memory_space_constraint(x, pltpu.VMEM) for x in arrays]


def far(*arrays):
    return [pltpu.with_memory_space_constraint(x, pltpu.HBM) for x in arrays]


def room(*shapes):
    held = sum(math.prod(shape) * jnp.dtype(dtype).itemsize for shape, dtype in shapes)
    return pltpu.CompilerParams(vmem_limit_bytes=2 * held + (1 << 20))


def project_kernel(acts, grads, p_in, p_out, out, x_v, w_v, sums, sems):
    for side, (x, w) in enumerate(((grads, p_out), (acts, p_in))):
        pltpu.make_async_copy(w, w_v.at[side], sems.at[side, 0]).start()
        pltpu.make_async_copy(x, x_v.at[side], sems.at[side, 1]).start()

    @pl.loop(0, 2)
    def _(side):
        pltpu.make_async_copy(p_in, w_v.at[side], sems.at[side, 0]).wait()
        pltpu.make_async_copy(acts, x_v.at[side], sems.at[side, 1]).wait()
        sums[side] = lax.dot_general(x_v[side], w_v[side], LAST, preferred_element_type=jnp.float32)

    out[...] = jnp.concatenate([sums[0], sums[1]], axis=1)


def project(acts, grads, p_in, p_out):
    rows, width = acts.shape
    proj = p_in.shape[0]
    bf16 = jnp.bfloat16
    return pl.pallas_call(
        project_kernel,
        out_shape=jax.ShapeDtypeStruct((rows, 2 * proj), jnp.float32),
        in_specs=[ANY] * 4,
        out_specs=VMEM,
        scratch_shapes=[
            pltpu.VMEM((2, rows, width), bf16),
            pltpu.VMEM((2, proj, width), bf16),
            pltpu.VMEM((2, rows, proj), jnp.float32),
            pltpu.SemaphoreType.DMA((2, 2)),
        ],
        compiler_params=room((acts.shape, bf16), (p_in.shape, bf16), ((rows, 4 * LANES), jnp.float32)),
        name="project",
    )(*far(acts, grads, p_in, p_out))


def rank(domains, row, first, named):
    fanout = domains.shape[0]
    found = jnp.int32(0)
    for other in range(first, row):
        if fanout <= 8:
            for k in range(fanout):
                found += (domains[k, other] == named).astype(jnp.int32)
        else:
            found = lax.fori_loop(
                0, fanout, lambda k, n, other=other: n + (domains[k, other] == named).astype(jnp.int32), found
            )
    return found


def feature_kernel(table, own, other, out, grams):
    fanout, seqs = table.shape
    length = own.shape[0] // seqs
    proj = own.shape[1] // 2
    half = out.shape[2]
    out[...] = jnp.zeros_like(out)
    both = own[...] + other[...]
    high = both.astype(jnp.bfloat16)
    low = (both - high.astype(jnp.float32)).astype(jnp.bfloat16)
    mine = lax.axis_index("tensor") * 2 * half
    left = lax.broadcasted_iota(jnp.int32, (half, LANES), 1) < proj
    for s in range(seqs):
        at = slice(s * length, (s + 1) * length)
        h, l = high[at], low[at]
        grams[s] = lax.dot_general(
            jnp.concatenate([h, l, h], axis=0)[:, :proj],
            jnp.concatenate([h, h, l], axis=0),
            (((0,), (0,)), ((), ())),
            preferred_element_type=jnp.float32,
        )
    for s in range(seqs):
        even = grams[s, pl.ds(mine, half, stride=2), :]
        odd = grams[s, pl.ds(mine + 1, half, stride=2), :]
        feature = jnp.where(left, pltpu.roll(even, proj, 1), odd).astype(out.dtype)

        def place(k, s=s, feature=feature):
            slot = table[k, s]
            out[slot // out.shape[1], slot % out.shape[1]] = feature

        each(fanout, place)


def spread(table, own, other, share, peers, tensor_count):
    seqs = table.shape[1]
    proj = own.shape[1] // 2
    half = proj * proj // LANES // tensor_count
    return pl.pallas_call(
        feature_kernel,
        out_shape=jax.ShapeDtypeStruct((peers, seqs // share * CAP, half, LANES), jnp.bfloat16),
        in_specs=[SMEM, VMEM, VMEM],
        out_specs=VMEM,
        scratch_shapes=[pltpu.VMEM((seqs, proj, 2 * proj), jnp.float32)],
        compiler_params=room(
            ((4 * own.shape[0], LANES), jnp.float32), ((peers, seqs // share * CAP, half, LANES), jnp.bfloat16)
        ),
        cost_estimate=pl.CostEstimate(flops=50_000_000_000, bytes_accessed=1 << 20, transcendentals=0),
        name="spread",
    )(table, *near(own, other))


def score_kernel(features, own, other, out, rows_v):
    peers, slots, half, _ = features.shape
    count = peers * slots
    rows_v[...] = features[...].reshape(count * half, LANES).astype(jnp.float32)
    rows = jnp.concatenate(
        [rows_v[pl.ds(c, count, stride=half), :].astype(jnp.bfloat16) for c in range(half)], axis=1
    )
    me = lax.axis_index("tensor")
    part = pl.ds(pl.multiple_of(me * half * LANES, LANES), half * LANES)
    mine, theirs = (
        lax.dot_general(rows, q[:, part], LAST, preferred_element_type=jnp.float32)
        for q in (own, other)
    )
    scores = jnp.concatenate([jnp.where(me == 0, mine, theirs), jnp.where(me == 0, theirs, mine)], axis=1)
    for p in range(out.shape[0]):
        out[p] = scores[p * CAP : (p + 1) * CAP]


def score(features, own, other):
    peers, slots, half, _ = features.shape
    return pl.pallas_call(
        score_kernel,
        out_shape=jax.ShapeDtypeStruct((peers * slots // CAP, CAP, 2 * own.shape[0]), jnp.float32),
        in_specs=[VMEM] * 3,
        out_specs=VMEM,
        scratch_shapes=[pltpu.VMEM((peers * slots * half, LANES), jnp.float32)],
        compiler_params=room(
            (features.shape, jnp.bfloat16),
            ((peers * slots * half, LANES), jnp.float32),
            ((2 * own.shape[0], own.shape[1]), jnp.bfloat16),
            ((peers * slots // CAP, 8, 2 * own.shape[0]), jnp.float32),
        ),
        name="score",
    )(*near(features, own, other))


def plan_kernel(share, domains, own, table):
    del own
    fanout, seqs = domains.shape
    groups = seqs // share
    for s in range(seqs):

        def place(k, s=s):
            named = domains[k, s]
            group = s // share
            table[k, s] = (named * groups + group) * CAP + rank(domains, s, group * share, named)

        each(fanout, place)


def plan(domains, own, share):
    return pl.pallas_call(
        functools.partial(plan_kernel, share),
        out_shape=pltpu.SMEM(domains.shape, jnp.int32),
        in_specs=[SMEM, ANY],
        out_specs=SMEM,
        compiler_params=room(),
        name="plan",
    )(domains, own)


def pick_kernel(table, scores, out):
    share, fanout, _ = out.shape
    halves = table.shape[1] // share
    first = lax.axis_index("tensor") * share
    for s in range(share):

        def take(k, s=s):
            slot = table[k, first + s]
            at = slot // (halves * CAP) * halves
            both = scores[at]
            for half in range(1, halves):
                both = both + scores[at + half]
            out[s, pl.ds(k, 1)] = jnp.where(slot % CAP == 0, both[0:1], both[1:2])

        each(fanout, take)


def pick(table, scores, share):
    return pl.pallas_call(
        pick_kernel,
        out_shape=jax.ShapeDtypeStruct((share, table.shape[0], scores.shape[2]), jnp.float32),
        in_specs=[SMEM, VMEM],
        out_specs=VMEM,
        compiler_params=room((scores.shape, jnp.float32), ((8 * share, table.shape[0], scores.shape[2]), jnp.float32)),
        name="pick",
    )(table, *near(scores))


def body(activations, out_grads, proj_in, proj_out, queries, domains):
    seqs, length, width = activations.shape
    peers = lax.axis_size("dp")
    tensor_count = lax.axis_size("tensor")
    share = seqs // tensor_count
    swap = [(i, i ^ 1) for i in range(tensor_count)]
    own = project(
        activations.reshape(seqs * length, width), out_grads.reshape(seqs * length, width), proj_in.T, proj_out.T
    )
    domains = domains.T
    other = lax.ppermute(own, "tensor", swap)
    table = plan(domains, own, share)
    queries, table = lax.optimization_barrier((queries, table))
    other_queries = lax.ppermute(queries, "tensor", swap)
    sent = spread(table, own, other, share, peers, tensor_count)
    came = lax.all_to_all(sent, "dp", split_axis=0, concat_axis=0, tiled=True)
    scores = score(came, queries, other_queries)
    back = lax.all_to_all(scores, ("dp", "tensor"), split_axis=0, concat_axis=0, tiled=True)
    return pick(table, back, share)


def solution(mesh):
    placed = (
        P(("groups", "dp"), None, "tensor"),
        P(("groups", "dp"), None, "tensor"),
        P("tensor", None),
        P("tensor", None),
        P(("groups", "dp", "tensor"), None),
        P(("groups", "dp"), None),
    )
    return jax.shard_map(
        body,
        mesh=mesh,
        in_specs=placed,
        out_specs=P(("groups", "dp", "tensor"), None, None),
        check_vma=False,
    )
```

```python
import functools
import math

import jax
import jax.numpy as jnp
from jax import lax
from jax.experimental import pallas as pl
from jax.experimental.pallas import tpu as pltpu
from jax.sharding import PartitionSpec as P

CAP = 2
LANES = 128
LAST = (((1,), (1,)), ((), ()))

VMEM = pl.BlockSpec(memory_space=pltpu.VMEM)
SMEM = pl.BlockSpec(memory_space=pltpu.SMEM)
ANY = pl.BlockSpec(memory_space=pl.ANY)


def turned(count, first):
    return [(first + i) % count for i in range(count)]


def each(count, step):
    if count <= 8:
        for at in range(count):
            step(at)
    else:
        lax.fori_loop(0, count, lambda at, _: (step(at), 0)[1], 0)


def near(*arrays):
    return [pltpu.with_memory_space_constraint(x, pltpu.VMEM) for x in arrays]


def far(*arrays):
    return [pltpu.with_memory_space_constraint(x, pltpu.HBM) for x in arrays]


def room(*shapes):
    held = sum(math.prod(shape) * jnp.dtype(dtype).itemsize for shape, dtype in shapes)
    return pltpu.CompilerParams(vmem_limit_bytes=2 * held + (1 << 20))


def project_kernel(acts, grads, p_in, p_out, out, x_v, w_v, sums, sems):
    for side, (x, w) in enumerate(((grads, p_out), (acts, p_in))):
        pltpu.make_async_copy(w, w_v.at[side], sems.at[side, 0]).start()
        pltpu.make_async_copy(x, x_v.at[side], sems.at[side, 1]).start()

    @pl.loop(0, 2)
    def _(side):
        pltpu.make_async_copy(p_in, w_v.at[side], sems.at[side, 0]).wait()
        pltpu.make_async_copy(acts, x_v.at[side], sems.at[side, 1]).wait()
        sums[side] = lax.dot_general(x_v[side], w_v[side], LAST, preferred_element_type=jnp.float32)

    out[...] = jnp.concatenate([sums[0], sums[1]], axis=1)


def project(acts, grads, p_in, p_out):
    rows, width = acts.shape
    proj = p_in.shape[0]
    bf16 = jnp.bfloat16
    return pl.pallas_call(
        project_kernel,
        out_shape=jax.ShapeDtypeStruct((rows, 2 * proj), jnp.float32),
        in_specs=[ANY] * 4,
        out_specs=VMEM,
        scratch_shapes=[
            pltpu.VMEM((2, rows, width), bf16),
            pltpu.VMEM((2, proj, width), bf16),
            pltpu.VMEM((2, rows, proj), jnp.float32),
            pltpu.SemaphoreType.DMA((2, 2)),
        ],
        compiler_params=room((acts.shape, bf16), (p_in.shape, bf16), ((rows, 4 * LANES), jnp.float32)),
        name="project",
    )(*far(acts, grads, p_in, p_out))


def rank(domains, row, first, named):
    fanout = domains.shape[0]
    found = jnp.int32(0)
    for other in range(first, row):
        if fanout <= 8:
            for k in range(fanout):
                found += (domains[k, other] == named).astype(jnp.int32)
        else:
            found = lax.fori_loop(
                0, fanout, lambda k, n, other=other: n + (domains[k, other] == named).astype(jnp.int32), found
            )
    return found


def feature_kernel(table, own, other, out, grams):
    fanout, seqs = table.shape
    length = own.shape[0] // seqs
    proj = own.shape[1] // 2
    half = out.shape[2]
    out[...] = jnp.zeros_like(out)
    both = own[...] + other[...]
    high = both.astype(jnp.bfloat16)
    low = (both - high.astype(jnp.float32)).astype(jnp.bfloat16)
    mine = lax.axis_index("tensor") * 2 * half
    left = lax.broadcasted_iota(jnp.int32, (half, LANES), 1) < proj
    for s in range(seqs):
        at = slice(s * length, (s + 1) * length)
        h, l = high[at], low[at]
        grams[s] = lax.dot_general(
            jnp.concatenate([h, l, h], axis=0)[:, :proj],
            jnp.concatenate([h, h, l], axis=0),
            (((0,), (0,)), ((), ())),
            preferred_element_type=jnp.float32,
        )
    for s in range(seqs):
        even = grams[s, pl.ds(mine, half, stride=2), :]
        odd = grams[s, pl.ds(mine + 1, half, stride=2), :]
        feature = jnp.where(left, pltpu.roll(even, proj, 1), odd).astype(out.dtype)

        def place(k, s=s, feature=feature):
            slot = table[k, s]
            out[slot // out.shape[1], slot % out.shape[1]] = feature

        each(fanout, place)


def spread(table, own, other, share, peers, tensor_count):
    seqs = table.shape[1]
    proj = own.shape[1] // 2
    half = proj * proj // LANES // tensor_count
    return pl.pallas_call(
        feature_kernel,
        out_shape=jax.ShapeDtypeStruct((peers, seqs // share * CAP, half, LANES), jnp.bfloat16),
        in_specs=[SMEM, VMEM, VMEM],
        out_specs=VMEM,
        scratch_shapes=[pltpu.VMEM((seqs, proj, 2 * proj), jnp.float32)],
        compiler_params=room(
            ((4 * own.shape[0], LANES), jnp.float32), ((peers, seqs // share * CAP, half, LANES), jnp.bfloat16)
        ),
        cost_estimate=pl.CostEstimate(flops=50_000_000_000, bytes_accessed=1 << 20, transcendentals=0),
        name="spread",
    )(table, *near(own, other))


def score_kernel(features, own, other, out, rows_v):
    peers, slots, half, _ = features.shape
    count = peers * slots
    rows_v[...] = features[...].reshape(count * half, LANES).astype(jnp.float32)
    rows = jnp.concatenate(
        [rows_v[pl.ds(c, count, stride=half), :].astype(jnp.bfloat16) for c in range(half)], axis=1
    )
    me = lax.axis_index("tensor")
    part = pl.ds(pl.multiple_of(me * half * LANES, LANES), half * LANES)
    mine, theirs = (
        lax.dot_general(rows, q[:, part], LAST, preferred_element_type=jnp.float32)
        for q in (own, other)
    )
    scores = jnp.concatenate([jnp.where(me == 0, mine, theirs), jnp.where(me == 0, theirs, mine)], axis=1)
    for p in range(out.shape[0]):
        out[(p - 1) % out.shape[0]] = scores[p * CAP : (p + 1) * CAP]


def score(features, own, other):
    peers, slots, half, _ = features.shape
    return pl.pallas_call(
        score_kernel,
        out_shape=jax.ShapeDtypeStruct((peers * slots // CAP, CAP, 2 * own.shape[0]), jnp.float32),
        in_specs=[VMEM] * 3,
        out_specs=VMEM,
        scratch_shapes=[pltpu.VMEM((peers * slots * half, LANES), jnp.float32)],
        compiler_params=room(
            (features.shape, jnp.bfloat16),
            ((peers * slots * half, LANES), jnp.float32),
            ((2 * own.shape[0], own.shape[1]), jnp.bfloat16),
            ((peers * slots // CAP, 8, 2 * own.shape[0]), jnp.float32),
        ),
        name="score",
    )(*near(features, own, other))


def plan_kernel(share, peers, meet, domains, own, table):
    del own
    fanout, seqs = domains.shape
    groups = seqs // share
    for s in range(seqs):

        def place(k, s=s):
            named = domains[k, s]
            group = s // share
            owner = (named + peers - meet) % peers
            table[k, s] = (owner * groups + group) * CAP + rank(domains, s, group * share, named)

        each(fanout, place)


def plan(domains, own, share, peers, meet):
    return pl.pallas_call(
        functools.partial(plan_kernel, share, peers, meet),
        out_shape=pltpu.SMEM(domains.shape, jnp.int32),
        in_specs=[SMEM, ANY],
        out_specs=SMEM,
        compiler_params=room(),
        name="plan",
    )(domains, own)


def pick_kernel(table, scores, out):
    share, fanout, _ = out.shape
    halves = table.shape[1] // share
    first = lax.axis_index("tensor") * share
    for s in range(share):

        def take(k, s=s):
            slot = table[k, first + s]
            at = slot // (halves * CAP) * halves + scores.shape[0] - 1
            both = scores[at % scores.shape[0]]
            for half in range(1, halves):
                both = both + scores[(at + half) % scores.shape[0]]
            out[s, pl.ds(k, 1)] = jnp.where(slot % CAP == 0, both[0:1], both[1:2])

        each(fanout, take)


def pick(table, scores, share):
    return pl.pallas_call(
        pick_kernel,
        out_shape=jax.ShapeDtypeStruct((share, table.shape[0], scores.shape[2]), jnp.float32),
        in_specs=[SMEM, VMEM],
        out_specs=VMEM,
        compiler_params=room((scores.shape, jnp.float32), ((8 * share, table.shape[0], scores.shape[2]), jnp.float32)),
        name="pick",
    )(table, *near(scores))


def body(activations, out_grads, proj_in, proj_out, queries, domains):
    seqs, length, width = activations.shape
    peers = lax.axis_size("dp")
    tensor_count = lax.axis_size("tensor")
    share = seqs // tensor_count
    swap = [(i, i ^ 1) for i in range(tensor_count)]
    meet = (peers // 2 + 1) % peers
    own = project(
        activations.reshape(seqs * length, width), out_grads.reshape(seqs * length, width), proj_in.T, proj_out.T
    )
    domains = domains.T
    other = lax.ppermute(own, "tensor", swap)
    table = plan(domains, own, share, peers, meet)
    queries, table = lax.optimization_barrier((queries, table))
    other_queries = lax.ppermute(queries, "tensor", swap)
    sent = spread(table, own, other, share, peers, tensor_count)
    came = lax.all_to_all(
        sent, "dp", split_axis=0, concat_axis=0, tiled=True, axis_index_groups=[turned(peers, meet)]
    )
    scores = score(came, queries, other_queries)
    devices = turned(peers * tensor_count, meet * tensor_count + 1)
    back = lax.all_to_all(
        scores, ("dp", "tensor"), split_axis=0, concat_axis=0, tiled=True, axis_index_groups=[devices]
    )
    return pick(table, back, share)


def solution(mesh):
    placed = (
        P(("groups", "dp"), None, "tensor"),
        P(("groups", "dp"), None, "tensor"),
        P("tensor", None),
        P("tensor", None),
        P(("groups", "dp", "tensor"), None),
        P(("groups", "dp"), None),
    )
    return jax.shard_map(
        body,
        mesh=mesh,
        in_specs=placed,
        out_specs=P(("groups", "dp", "tensor"), None, None),
        check_vma=False,
    )
```

```python
import functools
import math

import jax
import jax.numpy as jnp
from jax import lax
from jax.experimental import pallas as pl
from jax.experimental.pallas import tpu as pltpu
from jax.sharding import PartitionSpec as P

CAP = 2
LANES = 128
LAST = (((1,), (1,)), ((), ()))

VMEM = pl.BlockSpec(memory_space=pltpu.VMEM)
SMEM = pl.BlockSpec(memory_space=pltpu.SMEM)
ANY = pl.BlockSpec(memory_space=pl.ANY)


def half_of(index, core, peers):
    return core ^ (index >= peers // 2)


def my_half(peers):
    past = (lax.axis_index("dp") >= peers // 2).astype(jnp.int32)
    return lax.axis_index("tensor") ^ past


def turned(count, first):
    return [(first + i) % count for i in range(count)]


def each(count, step):
    if count <= 8:
        for at in range(count):
            step(at)
    else:
        lax.fori_loop(0, count, lambda at, _: (step(at), 0)[1], 0)


def near(*arrays):
    return [pltpu.with_memory_space_constraint(x, pltpu.VMEM) for x in arrays]


def far(*arrays):
    return [pltpu.with_memory_space_constraint(x, pltpu.HBM) for x in arrays]


def room(*shapes):
    held = sum(math.prod(shape) * jnp.dtype(dtype).itemsize for shape, dtype in shapes)
    return pltpu.CompilerParams(vmem_limit_bytes=2 * held + (1 << 20))


def project_kernel(acts, grads, p_in, p_out, out, x_v, w_v, sums, sems):
    for side, (x, w) in enumerate(((grads, p_out), (acts, p_in))):
        pltpu.make_async_copy(w, w_v.at[side], sems.at[side, 0]).start()
        pltpu.make_async_copy(x, x_v.at[side], sems.at[side, 1]).start()

    @pl.loop(0, 2)
    def _(side):
        pltpu.make_async_copy(p_in, w_v.at[side], sems.at[side, 0]).wait()
        pltpu.make_async_copy(acts, x_v.at[side], sems.at[side, 1]).wait()
        sums[side] = lax.dot_general(x_v[side], w_v[side], LAST, preferred_element_type=jnp.float32)

    out[...] = jnp.concatenate([sums[0], sums[1]], axis=1)


def project(acts, grads, p_in, p_out):
    rows, width = acts.shape
    proj = p_in.shape[0]
    bf16 = jnp.bfloat16
    return pl.pallas_call(
        project_kernel,
        out_shape=jax.ShapeDtypeStruct((rows, 2 * proj), jnp.float32),
        in_specs=[ANY] * 4,
        out_specs=VMEM,
        scratch_shapes=[
            pltpu.VMEM((2, rows, width), bf16),
            pltpu.VMEM((2, proj, width), bf16),
            pltpu.VMEM((2, rows, proj), jnp.float32),
            pltpu.SemaphoreType.DMA((2, 2)),
        ],
        compiler_params=room((acts.shape, bf16), (p_in.shape, bf16), ((rows, 4 * LANES), jnp.float32)),
        name="project",
    )(*far(acts, grads, p_in, p_out))


def rank(domains, row, first, named):
    fanout = domains.shape[0]
    found = jnp.int32(0)
    for other in range(first, row):
        if fanout <= 8:
            for k in range(fanout):
                found += (domains[k, other] == named).astype(jnp.int32)
        else:
            found = lax.fori_loop(
                0, fanout, lambda k, n, other=other: n + (domains[k, other] == named).astype(jnp.int32), found
            )
    return found


def feature_kernel(table, own, other, out, grams):
    fanout, seqs = table.shape
    length = own.shape[0] // seqs
    proj = own.shape[1] // 2
    half = out.shape[2]
    out[...] = jnp.zeros_like(out)
    both = own[...] + other[...]
    high = both.astype(jnp.bfloat16)
    low = (both - high.astype(jnp.float32)).astype(jnp.bfloat16)
    mine = my_half(out.shape[0]) * 2 * half
    left = lax.broadcasted_iota(jnp.int32, (half, LANES), 1) < proj
    for s in range(seqs):
        at = slice(s * length, (s + 1) * length)
        h, l = high[at], low[at]
        grams[s] = lax.dot_general(
            jnp.concatenate([h, l, h], axis=0)[:, :proj],
            jnp.concatenate([h, h, l], axis=0),
            (((0,), (0,)), ((), ())),
            preferred_element_type=jnp.float32,
        )
    for s in range(seqs):
        even = grams[s, pl.ds(mine, half, stride=2), :]
        odd = grams[s, pl.ds(mine + 1, half, stride=2), :]
        feature = jnp.where(left, pltpu.roll(even, proj, 1), odd).astype(out.dtype)

        def place(k, s=s, feature=feature):
            slot = table[k, s]
            out[slot // out.shape[1], slot % out.shape[1]] = feature

        each(fanout, place)


def spread(table, own, other, share, peers, tensor_count):
    seqs = table.shape[1]
    proj = own.shape[1] // 2
    half = proj * proj // LANES // tensor_count
    return pl.pallas_call(
        feature_kernel,
        out_shape=jax.ShapeDtypeStruct((peers, seqs // share * CAP, half, LANES), jnp.bfloat16),
        in_specs=[SMEM, VMEM, VMEM],
        out_specs=VMEM,
        scratch_shapes=[pltpu.VMEM((seqs, proj, 2 * proj), jnp.float32)],
        compiler_params=room(
            ((4 * own.shape[0], LANES), jnp.float32), ((peers, seqs // share * CAP, half, LANES), jnp.bfloat16)
        ),
        cost_estimate=pl.CostEstimate(flops=50_000_000_000, bytes_accessed=1 << 20, transcendentals=0),
        name="spread",
    )(table, *near(own, other))


def score_kernel(meet, features, own, other, out, rows_v):
    peers, slots, half, _ = features.shape
    count = peers * slots
    rows_v[...] = features[...].reshape(count * half, LANES).astype(jnp.float32)
    rows = jnp.concatenate(
        [rows_v[pl.ds(c, count, stride=half), :].astype(jnp.bfloat16) for c in range(half)], axis=1
    )
    me = lax.axis_index("tensor")
    part = pl.ds(pl.multiple_of(my_half(peers) * half * LANES, LANES), half * LANES)
    mine, theirs = (
        lax.dot_general(rows, q[:, part], LAST, preferred_element_type=jnp.float32)
        for q in (own, other)
    )
    scores = jnp.concatenate([jnp.where(me == 0, mine, theirs), jnp.where(me == 0, theirs, mine)], axis=1)
    devices = out.shape[0]
    for p in range(devices):
        out[(p + devices // peers * meet + 1) % devices] = scores[p * CAP : (p + 1) * CAP]


def score(features, own, other, meet):
    peers, slots, half, _ = features.shape
    return pl.pallas_call(
        functools.partial(score_kernel, meet),
        out_shape=jax.ShapeDtypeStruct((peers * slots // CAP, CAP, 2 * own.shape[0]), jnp.float32),
        in_specs=[VMEM] * 3,
        out_specs=VMEM,
        scratch_shapes=[pltpu.VMEM((peers * slots * half, LANES), jnp.float32)],
        compiler_params=room(
            (features.shape, jnp.bfloat16),
            ((peers * slots * half, LANES), jnp.float32),
            ((2 * own.shape[0], own.shape[1]), jnp.bfloat16),
            ((peers * slots // CAP, 8, 2 * own.shape[0]), jnp.float32),
        ),
        name="score",
    )(*near(features, own, other))


def plan_kernel(share, peers, meet, domains, own, table):
    del own
    fanout, seqs = domains.shape
    groups = seqs // share
    for s in range(seqs):

        def place(k, s=s):
            named = domains[k, s]
            group = s // share
            owner = (named + peers - meet) % peers
            table[k, s] = (owner * groups + group) * CAP + rank(domains, s, group * share, named)

        each(fanout, place)


def plan(domains, own, share, peers, meet):
    return pl.pallas_call(
        functools.partial(plan_kernel, share, peers, meet),
        out_shape=pltpu.SMEM(domains.shape, jnp.int32),
        in_specs=[SMEM, ANY],
        out_specs=SMEM,
        compiler_params=room(),
        name="plan",
    )(domains, own)


def pick_kernel(meet, table, scores, out):
    share, fanout, _ = out.shape
    halves = table.shape[1] // share
    first = lax.axis_index("tensor") * share
    for s in range(share):

        def take(k, s=s):
            slot = table[k, first + s]
            at = (slot // (halves * CAP) + meet) * halves + 1
            both = scores[at % scores.shape[0]]
            for half in range(1, halves):
                both = both + scores[(at + half) % scores.shape[0]]
            out[s, pl.ds(k, 1)] = jnp.where(slot % CAP == 0, both[0:1], both[1:2])

        each(fanout, take)


def pick(table, scores, share, meet):
    return pl.pallas_call(
        functools.partial(pick_kernel, meet),
        out_shape=jax.ShapeDtypeStruct((share, table.shape[0], scores.shape[2]), jnp.float32),
        in_specs=[SMEM, VMEM],
        out_specs=VMEM,
        compiler_params=room((scores.shape, jnp.float32), ((8 * share, table.shape[0], scores.shape[2]), jnp.float32)),
        name="pick",
    )(table, *near(scores))


def body(activations, out_grads, proj_in, proj_out, queries, domains):
    seqs, length, width = activations.shape
    peers = lax.axis_size("dp")
    tensor_count = lax.axis_size("tensor")
    share = seqs // tensor_count
    swap = [(i, i ^ 1) for i in range(tensor_count)]
    meet = (peers // 2 + 1) % peers
    own = project(
        activations.reshape(seqs * length, width), out_grads.reshape(seqs * length, width), proj_in.T, proj_out.T
    )
    domains = domains.T
    other = lax.ppermute(own, "tensor", swap)
    table = plan(domains, own, share, peers, meet)
    queries, table = lax.optimization_barrier((queries, table))
    other_queries = lax.ppermute(queries, "tensor", swap)
    sent = spread(table, own, other, share, peers, tensor_count)
    groups = [
        [index * tensor_count + half_of(index, half, peers) for index in turned(peers, meet)]
        for half in range(tensor_count)
    ]
    came = lax.all_to_all(
        sent, ("dp", "tensor"), split_axis=0, concat_axis=0, tiled=True, axis_index_groups=groups
    )
    scores = score(came, queries, other_queries, meet)
    devices = peers * tensor_count
    back = lax.all_to_all(
        scores,
        ("dp", "tensor"),
        split_axis=0,
        concat_axis=0,
        tiled=True,
        axis_index_groups=[turned(devices, devices - 1)],
    )
    return pick(table, back, share, meet)


def solution(mesh):
    placed = (
        P(("groups", "dp"), None, "tensor"),
        P(("groups", "dp"), None, "tensor"),
        P("tensor", None),
        P("tensor", None),
        P(("groups", "dp", "tensor"), None),
        P(("groups", "dp"), None),
    )
    return jax.shard_map(
        body,
        mesh=mesh,
        in_specs=placed,
        out_specs=P(("groups", "dp", "tensor"), None, None),
        check_vma=False,
    )
```

```python
import functools
import math

import jax
import jax.numpy as jnp
from jax import lax
from jax.experimental import pallas as pl
from jax.experimental.pallas import tpu as pltpu
from jax.sharding import PartitionSpec as P

CAP = 2
LANES = 128
LAST = (((1,), (1,)), ((), ()))

VMEM = pl.BlockSpec(memory_space=pltpu.VMEM)
SMEM = pl.BlockSpec(memory_space=pltpu.SMEM)
ANY = pl.BlockSpec(memory_space=pl.ANY)


def half_of(index, core, peers):
    return core ^ (index >= peers // 2)


def my_half(peers):
    past = (lax.axis_index("dp") >= peers // 2).astype(jnp.int32)
    return lax.axis_index("tensor") ^ past


def turned(count, first):
    return [(first + i) % count for i in range(count)]


def each(count, step):
    if count <= 8:
        for at in range(count):
            step(at)
    else:
        lax.fori_loop(0, count, lambda at, _: (step(at), 0)[1], 0)


def near(*arrays):
    return [pltpu.with_memory_space_constraint(x, pltpu.VMEM) for x in arrays]


def far(*arrays):
    return [pltpu.with_memory_space_constraint(x, pltpu.HBM) for x in arrays]


def room(*shapes):
    held = sum(math.prod(shape) * jnp.dtype(dtype).itemsize for shape, dtype in shapes)
    return pltpu.CompilerParams(vmem_limit_bytes=2 * held + (1 << 20))


def project_kernel(acts, grads, p_in, p_out, out, x_v, w_v, sums, sems):
    for side, (x, w) in enumerate(((grads, p_out), (acts, p_in))):
        pltpu.make_async_copy(w, w_v.at[side], sems.at[side, 0]).start()
        pltpu.make_async_copy(x, x_v.at[side], sems.at[side, 1]).start()

    @pl.loop(0, 2)
    def _(side):
        pltpu.make_async_copy(p_in, w_v.at[side], sems.at[side, 0]).wait()
        pltpu.make_async_copy(acts, x_v.at[side], sems.at[side, 1]).wait()
        sums[side] = lax.dot_general(x_v[side], w_v[side], LAST, preferred_element_type=jnp.float32)

    out[...] = jnp.concatenate([sums[0], sums[1]], axis=1)


def project(acts, grads, p_in, p_out):
    rows, width = acts.shape
    proj = p_in.shape[0]
    bf16 = jnp.bfloat16
    return pl.pallas_call(
        project_kernel,
        out_shape=jax.ShapeDtypeStruct((rows, 2 * proj), jnp.float32),
        in_specs=[ANY] * 4,
        out_specs=VMEM,
        scratch_shapes=[
            pltpu.VMEM((2, rows, width), bf16),
            pltpu.VMEM((2, proj, width), bf16),
            pltpu.VMEM((2, rows, proj), jnp.float32),
            pltpu.SemaphoreType.DMA((2, 2)),
        ],
        compiler_params=room((acts.shape, bf16), (p_in.shape, bf16), ((rows, 4 * LANES), jnp.float32)),
        name="project",
    )(*far(acts, grads, p_in, p_out))


def rank(domains, row, first, named):
    fanout = domains.shape[0]
    found = jnp.int32(0)
    for other in range(first, row):
        if fanout <= 8:
            for k in range(fanout):
                found += (domains[k, other] == named).astype(jnp.int32)
        else:
            found = lax.fori_loop(
                0, fanout, lambda k, n, other=other: n + (domains[k, other] == named).astype(jnp.int32), found
            )
    return found


def feature_kernel(table, own, other, out, grams):
    fanout, seqs = table.shape
    length = own.shape[0] // seqs
    proj = own.shape[1] // 2
    half = out.shape[2]
    out[...] = jnp.zeros_like(out)
    both = own[...] + other[...]
    high = both.astype(jnp.bfloat16)
    low = (both - high.astype(jnp.float32)).astype(jnp.bfloat16)
    mine = my_half(out.shape[0]) * 2 * half
    left = lax.broadcasted_iota(jnp.int32, (half, LANES), 1) < proj
    for s in range(seqs):
        at = slice(s * length, (s + 1) * length)
        h, l = high[at], low[at]
        grams[s] = lax.dot_general(
            jnp.concatenate([h, l, h, l], axis=0)[:, :proj],
            jnp.concatenate([h, h, l, l], axis=0),
            (((0,), (0,)), ((), ())),
            preferred_element_type=jnp.float32,
        )
    for s in range(seqs):
        even = grams[s, pl.ds(mine, half, stride=2), :]
        odd = grams[s, pl.ds(mine + 1, half, stride=2), :]
        feature = jnp.where(left, pltpu.roll(even, proj, 1), odd).astype(out.dtype)

        def place(k, s=s, feature=feature):
            slot = table[k, s]
            out[slot // out.shape[1], slot % out.shape[1]] = feature

        each(fanout, place)


def spread(table, own, other, share, peers, tensor_count):
    seqs = table.shape[1]
    proj = own.shape[1] // 2
    half = proj * proj // LANES // tensor_count
    return pl.pallas_call(
        feature_kernel,
        out_shape=jax.ShapeDtypeStruct((peers, seqs // share * CAP, half, LANES), jnp.bfloat16),
        in_specs=[SMEM, VMEM, VMEM],
        out_specs=VMEM,
        scratch_shapes=[pltpu.VMEM((seqs, proj, 2 * proj), jnp.float32)],
        compiler_params=room(
            ((4 * own.shape[0], LANES), jnp.float32), ((peers, seqs // share * CAP, half, LANES), jnp.bfloat16)
        ),
        cost_estimate=pl.CostEstimate(flops=50_000_000_000, bytes_accessed=1 << 20, transcendentals=0),
        name="spread",
    )(table, *near(own, other))


def score_kernel(meet, features, own, other, out, rows_v):
    peers, slots, half, _ = features.shape
    count = peers * slots
    rows_v[...] = features[...].reshape(count * half, LANES).astype(jnp.float32)
    rows = jnp.concatenate(
        [rows_v[pl.ds(c, count, stride=half), :].astype(jnp.bfloat16) for c in range(half)], axis=1
    )
    me = lax.axis_index("tensor")
    part = pl.ds(pl.multiple_of(my_half(peers) * half * LANES, LANES), half * LANES)
    mine, theirs = (
        lax.dot_general(q[:, part], rows, LAST, preferred_element_type=jnp.float32)
        for q in (own, other)
    )
    scores = jnp.concatenate([jnp.where(me == 0, mine, theirs), jnp.where(me == 0, theirs, mine)], axis=0).T
    devices = out.shape[0]
    for p in range(devices):
        out[(p + devices // peers * meet + 1) % devices] = scores[p * CAP : (p + 1) * CAP]


def score(features, own, other, meet):
    peers, slots, half, _ = features.shape
    return pl.pallas_call(
        functools.partial(score_kernel, meet),
        out_shape=jax.ShapeDtypeStruct((peers * slots // CAP, CAP, 2 * own.shape[0]), jnp.float32),
        in_specs=[VMEM] * 3,
        out_specs=VMEM,
        scratch_shapes=[pltpu.VMEM((peers * slots * half, LANES), jnp.float32)],
        compiler_params=room(
            (features.shape, jnp.bfloat16),
            ((peers * slots * half, LANES), jnp.float32),
            ((2 * own.shape[0], own.shape[1]), jnp.bfloat16),
            ((peers * slots // CAP, 8, 2 * own.shape[0]), jnp.float32),
        ),
        name="score",
    )(*near(features, own, other))


def plan_kernel(share, peers, meet, domains, own, table):
    del own
    fanout, seqs = domains.shape
    groups = seqs // share
    for s in range(seqs):

        def place(k, s=s):
            named = domains[k, s]
            group = s // share
            owner = (named + peers - meet) % peers
            table[k, s] = (owner * groups + group) * CAP + rank(domains, s, group * share, named)

        each(fanout, place)


def plan(domains, own, share, peers, meet):
    return pl.pallas_call(
        functools.partial(plan_kernel, share, peers, meet),
        out_shape=pltpu.SMEM(domains.shape, jnp.int32),
        in_specs=[SMEM, ANY],
        out_specs=SMEM,
        compiler_params=room(),
        name="plan",
    )(domains, own)


def pick_kernel(meet, table, scores, out):
    share, fanout, _ = out.shape
    halves = table.shape[1] // share
    first = lax.axis_index("tensor") * share
    for s in range(share):

        def take(k, s=s):
            slot = table[k, first + s]
            at = (slot // (halves * CAP) + meet) * halves + 1
            both = scores[at % scores.shape[0]]
            for half in range(1, halves):
                both = both + scores[(at + half) % scores.shape[0]]
            out[s, pl.ds(k, 1)] = jnp.where(slot % CAP == 0, both[0:1], both[1:2])

        each(fanout, take)


def pick(table, scores, share, meet):
    return pl.pallas_call(
        functools.partial(pick_kernel, meet),
        out_shape=jax.ShapeDtypeStruct((share, table.shape[0], scores.shape[2]), jnp.float32),
        in_specs=[SMEM, VMEM],
        out_specs=VMEM,
        compiler_params=room((scores.shape, jnp.float32), ((8 * share, table.shape[0], scores.shape[2]), jnp.float32)),
        name="pick",
    )(table, *near(scores))


def body(activations, out_grads, proj_in, proj_out, queries, domains):
    seqs, length, width = activations.shape
    peers = lax.axis_size("dp")
    tensor_count = lax.axis_size("tensor")
    share = seqs // tensor_count
    swap = [(i, i ^ 1) for i in range(tensor_count)]
    meet = (peers // 2 + 1) % peers
    own = project(
        activations.reshape(seqs * length, width), out_grads.reshape(seqs * length, width), proj_in.T, proj_out.T
    )
    domains = domains.T
    other = lax.ppermute(own, "tensor", swap)
    table = plan(domains, own, share, peers, meet)
    kept, table = lax.optimization_barrier((queries, table))
    queries, own = lax.optimization_barrier((queries, own))
    other_queries = lax.ppermute(queries, "tensor", swap)
    queries = kept
    sent = spread(table, own, other, share, peers, tensor_count)
    groups = [
        [index * tensor_count + half_of(index, half, peers) for index in turned(peers, meet)]
        for half in range(tensor_count)
    ]
    came = lax.all_to_all(
        sent, ("dp", "tensor"), split_axis=0, concat_axis=0, tiled=True, axis_index_groups=groups
    )
    scores = score(came, queries, other_queries, meet)
    devices = peers * tensor_count
    back = lax.all_to_all(
        scores,
        ("dp", "tensor"),
        split_axis=0,
        concat_axis=0,
        tiled=True,
        axis_index_groups=[turned(devices, devices - 1)],
    )
    return pick(table, back, share, meet)


def solution(mesh):
    placed = (
        P(("groups", "dp"), None, "tensor"),
        P(("groups", "dp"), None, "tensor"),
        P("tensor", None),
        P("tensor", None),
        P(("groups", "dp", "tensor"), None),
        P(("groups", "dp"), None),
    )
    return jax.shard_map(
        body,
        mesh=mesh,
        in_specs=placed,
        out_specs=P(("groups", "dp", "tensor"), None, None),
        check_vma=False,
    )
```

```python
import functools
import math

import jax
import jax.numpy as jnp
from jax import lax
from jax.experimental import pallas as pl
from jax.experimental.pallas import tpu as pltpu
from jax.sharding import PartitionSpec as P

CAP = 2
LANES = 128
LAST = (((1,), (1,)), ((), ()))

VMEM = pl.BlockSpec(memory_space=pltpu.VMEM)
SMEM = pl.BlockSpec(memory_space=pltpu.SMEM)
ANY = pl.BlockSpec(memory_space=pl.ANY)


def half_of(index, core, peers):
    return core ^ (index >= peers // 2)


def my_half(peers):
    past = (lax.axis_index("dp") >= peers // 2).astype(jnp.int32)
    return lax.axis_index("tensor") ^ past


def turned(count, first):
    return [(first + i) % count for i in range(count)]


def each(count, step):
    if count <= 8:
        for at in range(count):
            step(at)
    else:
        lax.fori_loop(0, count, lambda at, _: (step(at), 0)[1], 0)


def near(*arrays):
    return [pltpu.with_memory_space_constraint(x, pltpu.VMEM) for x in arrays]


def far(*arrays):
    return [pltpu.with_memory_space_constraint(x, pltpu.HBM) for x in arrays]


def room(*shapes):
    held = sum(math.prod(shape) * jnp.dtype(dtype).itemsize for shape, dtype in shapes)
    return pltpu.CompilerParams(vmem_limit_bytes=2 * held + (1 << 20))


def project_kernel(acts, grads, p_in, p_out, out, x_v, w_v, sems):
    proj = p_in.shape[0]
    for side, (x, w) in enumerate(((grads, p_out), (acts, p_in))):
        pltpu.make_async_copy(w, w_v.at[side, pl.ds(side * proj, proj)], sems.at[side, 0]).start()
        pltpu.make_async_copy(x, x_v.at[side], sems.at[side, 1]).start()
    for side in range(2):
        w_v[side, pl.ds((1 - side) * proj, proj)] = jnp.zeros(p_in.shape, w_v.dtype)
    out[...] = jnp.zeros_like(out)

    @pl.loop(0, 2)
    def _(side):
        pltpu.make_async_copy(p_in, w_v.at[side, pl.ds(pl.multiple_of(side * proj, proj), proj)], sems.at[side, 0]).wait()
        pltpu.make_async_copy(acts, x_v.at[side], sems.at[side, 1]).wait()
        out[...] += lax.dot_general(x_v[side], w_v[side], LAST, preferred_element_type=jnp.float32)


def project(acts, grads, p_in, p_out):
    rows, width = acts.shape
    proj = p_in.shape[0]
    bf16 = jnp.bfloat16
    return pl.pallas_call(
        project_kernel,
        out_shape=jax.ShapeDtypeStruct((rows, 2 * proj), jnp.float32),
        in_specs=[ANY] * 4,
        out_specs=VMEM,
        scratch_shapes=[
            pltpu.VMEM((2, rows, width), bf16),
            pltpu.VMEM((2, 2 * proj, width), bf16),
            pltpu.SemaphoreType.DMA((2, 2)),
        ],
        compiler_params=room((acts.shape, bf16), ((4 * proj, width), bf16), ((rows, 2 * LANES), jnp.float32)),
        name="project",
    )(*far(acts, grads, p_in, p_out))


def rank(domains, row, first, named):
    fanout = domains.shape[0]
    found = jnp.int32(0)
    for other in range(first, row):
        if fanout <= 8:
            for k in range(fanout):
                found += (domains[k, other] == named).astype(jnp.int32)
        else:
            found = lax.fori_loop(
                0, fanout, lambda k, n, other=other: n + (domains[k, other] == named).astype(jnp.int32), found
            )
    return found


def feature_kernel(table, own, other, out, grams):
    fanout, seqs = table.shape
    length = own.shape[0] // seqs
    proj = own.shape[1] // 2
    half = out.shape[2]
    out[...] = jnp.zeros_like(out)
    both = own[...] + other[...]
    high = both.astype(jnp.bfloat16)
    low = (both - high.astype(jnp.float32)).astype(jnp.bfloat16)
    mine = my_half(out.shape[0]) * 2 * half
    left = lax.broadcasted_iota(jnp.int32, (half, LANES), 1) < proj
    for s in range(seqs):
        at = slice(s * length, (s + 1) * length)
        h, l = high[at], low[at]
        grams[s] = lax.dot_general(
            jnp.concatenate([h, l, h, l], axis=0)[:, :proj],
            jnp.concatenate([h, h, l, l], axis=0),
            (((0,), (0,)), ((), ())),
            preferred_element_type=jnp.float32,
        )
    for s in range(seqs):
        even = grams[s, pl.ds(mine, half, stride=2), :]
        odd = grams[s, pl.ds(mine + 1, half, stride=2), :]
        feature = jnp.where(left, pltpu.roll(even, proj, 1), odd).astype(out.dtype)

        def place(k, s=s, feature=feature):
            slot = table[k, s]
            out[slot // out.shape[1], slot % out.shape[1]] = feature

        each(fanout, place)


def spread(table, own, other, share, peers, tensor_count):
    seqs = table.shape[1]
    proj = own.shape[1] // 2
    half = proj * proj // LANES // tensor_count
    return pl.pallas_call(
        feature_kernel,
        out_shape=jax.ShapeDtypeStruct((peers, seqs // share * CAP, half, LANES), jnp.bfloat16),
        in_specs=[SMEM, VMEM, VMEM],
        out_specs=VMEM,
        scratch_shapes=[pltpu.VMEM((seqs, proj, 2 * proj), jnp.float32)],
        compiler_params=room(
            ((4 * own.shape[0], LANES), jnp.float32), ((peers, seqs // share * CAP, half, LANES), jnp.bfloat16)
        ),
        cost_estimate=pl.CostEstimate(flops=50_000_000_000, bytes_accessed=1 << 20, transcendentals=0),
        name="spread",
    )(table, *near(own, other))


def score_kernel(meet, features, own, other, out, rows_v):
    peers, slots, half, _ = features.shape
    count = peers * slots
    rows_v[...] = features[...].reshape(count * half, LANES).astype(jnp.float32)
    rows = jnp.concatenate(
        [rows_v[pl.ds(c, count, stride=half), :].astype(jnp.bfloat16) for c in range(half)], axis=1
    )
    me = lax.axis_index("tensor")
    part = pl.ds(pl.multiple_of(my_half(peers) * half * LANES, LANES), half * LANES)
    mine, theirs = (
        lax.dot_general(q[:, part], rows, LAST, preferred_element_type=jnp.float32)
        for q in (own, other)
    )
    scores = jnp.concatenate([jnp.where(me == 0, mine, theirs), jnp.where(me == 0, theirs, mine)], axis=0).T
    devices = out.shape[0]
    for p in range(devices):
        out[(p + devices // peers * meet + 1) % devices] = scores[p * CAP : (p + 1) * CAP]


def score(features, own, other, meet):
    peers, slots, half, _ = features.shape
    return pl.pallas_call(
        functools.partial(score_kernel, meet),
        out_shape=jax.ShapeDtypeStruct((peers * slots // CAP, CAP, 2 * own.shape[0]), jnp.float32),
        in_specs=[VMEM] * 3,
        out_specs=VMEM,
        scratch_shapes=[pltpu.VMEM((peers * slots * half, LANES), jnp.float32)],
        compiler_params=room(
            (features.shape, jnp.bfloat16),
            ((peers * slots * half, LANES), jnp.float32),
            ((2 * own.shape[0], own.shape[1]), jnp.bfloat16),
            ((peers * slots // CAP, 8, 2 * own.shape[0]), jnp.float32),
        ),
        name="score",
    )(*near(features, own, other))


def plan_kernel(share, peers, meet, domains, own, table):
    del own
    fanout, seqs = domains.shape
    groups = seqs // share
    for s in range(seqs):

        def place(k, s=s):
            named = domains[k, s]
            group = s // share
            owner = (named + peers - meet) % peers
            table[k, s] = (owner * groups + group) * CAP + rank(domains, s, group * share, named)

        each(fanout, place)


def plan(domains, own, share, peers, meet):
    return pl.pallas_call(
        functools.partial(plan_kernel, share, peers, meet),
        out_shape=pltpu.SMEM(domains.shape, jnp.int32),
        in_specs=[SMEM, ANY],
        out_specs=SMEM,
        compiler_params=room(),
        name="plan",
    )(domains, own)


def pick_kernel(meet, table, scores, out):
    share, fanout, _ = out.shape
    halves = table.shape[1] // share
    first = lax.axis_index("tensor") * share
    for s in range(share):

        def take(k, s=s):
            slot = table[k, first + s]
            at = (slot // (halves * CAP) + meet) * halves + 1
            both = scores[at % scores.shape[0]]
            for half in range(1, halves):
                both = both + scores[(at + half) % scores.shape[0]]
            out[s, pl.ds(k, 1)] = jnp.where(slot % CAP == 0, both[0:1], both[1:2])

        each(fanout, take)


def pick(table, scores, share, meet):
    return pl.pallas_call(
        functools.partial(pick_kernel, meet),
        out_shape=jax.ShapeDtypeStruct((share, table.shape[0], scores.shape[2]), jnp.float32),
        in_specs=[SMEM, VMEM],
        out_specs=VMEM,
        compiler_params=room((scores.shape, jnp.float32), ((8 * share, table.shape[0], scores.shape[2]), jnp.float32)),
        name="pick",
    )(table, *near(scores))


def body(activations, out_grads, proj_in, proj_out, queries, domains):
    seqs, length, width = activations.shape
    peers = lax.axis_size("dp")
    tensor_count = lax.axis_size("tensor")
    share = seqs // tensor_count
    swap = [(i, i ^ 1) for i in range(tensor_count)]
    meet = (peers // 2 + 1) % peers
    own = project(
        activations.reshape(seqs * length, width), out_grads.reshape(seqs * length, width), proj_in.T, proj_out.T
    )
    domains = domains.T
    other = lax.ppermute(own, "tensor", swap)
    table = plan(domains, own, share, peers, meet)
    kept, table = lax.optimization_barrier((queries, table))
    queries, own = lax.optimization_barrier((queries, own))
    other_queries = lax.ppermute(queries, "tensor", swap)
    queries = kept
    sent = spread(table, own, other, share, peers, tensor_count)
    groups = [
        [index * tensor_count + half_of(index, half, peers) for index in turned(peers, meet)]
        for half in range(tensor_count)
    ]
    came = lax.all_to_all(
        sent, ("dp", "tensor"), split_axis=0, concat_axis=0, tiled=True, axis_index_groups=groups
    )
    scores = score(came, queries, other_queries, meet)
    devices = peers * tensor_count
    back = lax.all_to_all(
        scores,
        ("dp", "tensor"),
        split_axis=0,
        concat_axis=0,
        tiled=True,
        axis_index_groups=[turned(devices, devices - 1)],
    )
    return pick(table, back, share, meet)


def solution(mesh):
    placed = (
        P(("groups", "dp"), None, "tensor"),
        P(("groups", "dp"), None, "tensor"),
        P("tensor", None),
        P("tensor", None),
        P(("groups", "dp", "tensor"), None),
        P(("groups", "dp"), None),
    )
    return jax.shard_map(
        body,
        mesh=mesh,
        in_specs=placed,
        out_specs=P(("groups", "dp", "tensor"), None, None),
        check_vma=False,
    )
```

```python
import functools
import math

import jax
import jax.numpy as jnp
from jax import lax
from jax.experimental import pallas as pl
from jax.experimental.pallas import tpu as pltpu
from jax.sharding import PartitionSpec as P

CAP = 2
LANES = 128
LAST = (((1,), (1,)), ((), ()))

VMEM = pl.BlockSpec(memory_space=pltpu.VMEM)
SMEM = pl.BlockSpec(memory_space=pltpu.SMEM)
ANY = pl.BlockSpec(memory_space=pl.ANY)


def half_of(index, core, peers):
    return core ^ (index >= peers // 2)


def my_half(peers):
    past = (lax.axis_index("dp") >= peers // 2).astype(jnp.int32)
    return lax.axis_index("tensor") ^ past


def turned(count, first):
    return [(first + i) % count for i in range(count)]


def each(count, step):
    if count <= 8:
        for at in range(count):
            step(at)
    else:
        lax.fori_loop(0, count, lambda at, _: (step(at), 0)[1], 0)


def near(*arrays):
    return [pltpu.with_memory_space_constraint(x, pltpu.VMEM) for x in arrays]


def far(*arrays):
    return [pltpu.with_memory_space_constraint(x, pltpu.HBM) for x in arrays]


def room(*shapes):
    held = sum(math.prod(shape) * jnp.dtype(dtype).itemsize for shape, dtype in shapes)
    return pltpu.CompilerParams(vmem_limit_bytes=2 * held + (1 << 20))


def project_kernel(acts, grads, p_in, p_out, out, x_v, w_v, sems):
    proj = p_in.shape[0]
    for side, (x, w) in enumerate(((grads, p_out), (acts, p_in))):
        pltpu.make_async_copy(x, x_v.at[side], sems.at[side, 1]).start()
        pltpu.make_async_copy(w, w_v.at[side, pl.ds(side * proj, proj)], sems.at[side, 0]).start()
    for side in range(2):
        w_v[side, pl.ds((1 - side) * proj, proj)] = jnp.zeros(p_in.shape, w_v.dtype)
    out[...] = jnp.zeros_like(out)

    @pl.loop(0, 2)
    def _(side):
        pltpu.make_async_copy(p_in, w_v.at[side, pl.ds(pl.multiple_of(side * proj, proj), proj)], sems.at[side, 0]).wait()
        pltpu.make_async_copy(acts, x_v.at[side], sems.at[side, 1]).wait()
        out[...] += lax.dot_general(x_v[side], w_v[side], LAST, preferred_element_type=jnp.float32)


def project(acts, grads, p_in, p_out):
    rows, width = acts.shape
    proj = p_in.shape[0]
    bf16 = jnp.bfloat16
    return pl.pallas_call(
        project_kernel,
        out_shape=jax.ShapeDtypeStruct((rows, 2 * proj), jnp.float32),
        in_specs=[ANY] * 4,
        out_specs=VMEM,
        scratch_shapes=[
            pltpu.VMEM((2, rows, width), bf16),
            pltpu.VMEM((2, 2 * proj, width), bf16),
            pltpu.SemaphoreType.DMA((2, 2)),
        ],
        compiler_params=room((acts.shape, bf16), ((4 * proj, width), bf16), ((rows, 2 * LANES), jnp.float32)),
        name="project",
    )(*far(acts, grads, p_in, p_out))


def rank(domains, row, first, named):
    fanout = domains.shape[0]
    found = jnp.int32(0)
    for other in range(first, row):
        if fanout <= 8:
            for k in range(fanout):
                found += (domains[k, other] == named).astype(jnp.int32)
        else:
            found = lax.fori_loop(
                0, fanout, lambda k, n, other=other: n + (domains[k, other] == named).astype(jnp.int32), found
            )
    return found


def feature_kernel(table, own, other, out, grams):
    fanout, seqs = table.shape
    length = own.shape[0] // seqs
    proj = own.shape[1] // 2
    half = out.shape[2]
    out[...] = jnp.zeros_like(out)
    both = own[...] + other[...]
    high = both.astype(jnp.bfloat16)
    low = (both - high.astype(jnp.float32)).astype(jnp.bfloat16)
    mine = my_half(out.shape[0]) * 2 * half
    left = lax.broadcasted_iota(jnp.int32, (half, LANES), 1) < proj
    for s in range(seqs):
        at = slice(s * length, (s + 1) * length)
        h, l = high[at], low[at]
        grams[s] = lax.dot_general(
            jnp.concatenate([h, l, h, l], axis=0)[:, :proj],
            jnp.concatenate([h, h, l, l], axis=0),
            (((0,), (0,)), ((), ())),
            preferred_element_type=jnp.float32,
        )
    for s in range(seqs):
        even = grams[s, pl.ds(mine, half, stride=2), :]
        odd = grams[s, pl.ds(mine + 1, half, stride=2), :]
        feature = jnp.where(left, pltpu.roll(even, proj, 1), odd).astype(out.dtype)

        def place(k, s=s, feature=feature):
            slot = table[k, s]
            out[slot // out.shape[1], slot % out.shape[1]] = feature

        each(fanout, place)


def spread(table, own, other, share, peers, tensor_count):
    seqs = table.shape[1]
    proj = own.shape[1] // 2
    half = proj * proj // LANES // tensor_count
    return pl.pallas_call(
        feature_kernel,
        out_shape=jax.ShapeDtypeStruct((peers, seqs // share * CAP, half, LANES), jnp.bfloat16),
        in_specs=[SMEM, VMEM, VMEM],
        out_specs=VMEM,
        scratch_shapes=[pltpu.VMEM((seqs, proj, 2 * proj), jnp.float32)],
        compiler_params=room(
            ((4 * own.shape[0], LANES), jnp.float32), ((peers, seqs // share * CAP, half, LANES), jnp.bfloat16)
        ),
        cost_estimate=pl.CostEstimate(flops=50_000_000_000, bytes_accessed=1 << 20, transcendentals=0),
        name="spread",
    )(table, *near(own, other))


def score_kernel(meet, features, own, other, out, rows_v):
    peers, slots, half, _ = features.shape
    count = peers * slots
    rows_v[...] = features[...].reshape(count * half, LANES).astype(jnp.float32)
    rows = jnp.concatenate(
        [rows_v[pl.ds(c, count, stride=half), :].astype(jnp.bfloat16) for c in range(half)], axis=1
    )
    me = lax.axis_index("tensor")
    part = pl.ds(pl.multiple_of(my_half(peers) * half * LANES, LANES), half * LANES)
    mine, theirs = (
        lax.dot_general(q[:, part], rows, LAST, preferred_element_type=jnp.float32)
        for q in (own, other)
    )
    scores = jnp.concatenate([jnp.where(me == 0, mine, theirs), jnp.where(me == 0, theirs, mine)], axis=0).T
    devices = out.shape[0]
    for p in range(devices):
        out[(p + devices // peers * meet + 1) % devices] = scores[p * CAP : (p + 1) * CAP]


def score(features, own, other, meet):
    peers, slots, half, _ = features.shape
    return pl.pallas_call(
        functools.partial(score_kernel, meet),
        out_shape=jax.ShapeDtypeStruct((peers * slots // CAP, CAP, 2 * own.shape[0]), jnp.float32),
        in_specs=[VMEM] * 3,
        out_specs=VMEM,
        scratch_shapes=[pltpu.VMEM((peers * slots * half, LANES), jnp.float32)],
        compiler_params=room(
            (features.shape, jnp.bfloat16),
            ((peers * slots * half, LANES), jnp.float32),
            ((2 * own.shape[0], own.shape[1]), jnp.bfloat16),
            ((peers * slots // CAP, 8, 2 * own.shape[0]), jnp.float32),
        ),
        name="score",
    )(*near(features, own, other))


def plan_kernel(share, peers, meet, domains, own, table):
    del own
    fanout, seqs = domains.shape
    groups = seqs // share
    for s in range(seqs):

        def place(k, s=s):
            named = domains[k, s]
            group = s // share
            owner = (named + peers - meet) % peers
            table[k, s] = (owner * groups + group) * CAP + rank(domains, s, group * share, named)

        each(fanout, place)


def plan(domains, own, share, peers, meet):
    return pl.pallas_call(
        functools.partial(plan_kernel, share, peers, meet),
        out_shape=pltpu.SMEM(domains.shape, jnp.int32),
        in_specs=[SMEM, ANY],
        out_specs=SMEM,
        compiler_params=room(),
        name="plan",
    )(domains, own)


def pick_kernel(meet, table, scores, out):
    share, fanout, _ = out.shape
    halves = table.shape[1] // share
    first = lax.axis_index("tensor") * share
    for s in range(share):

        def take(k, s=s):
            slot = table[k, first + s]
            at = (slot // (halves * CAP) + meet) * halves + 1
            both = scores[at % scores.shape[0]]
            for half in range(1, halves):
                both = both + scores[(at + half) % scores.shape[0]]
            out[s, pl.ds(k, 1)] = jnp.where(slot % CAP == 0, both[0:1], both[1:2])

        each(fanout, take)


def pick(table, scores, share, meet):
    return pl.pallas_call(
        functools.partial(pick_kernel, meet),
        out_shape=jax.ShapeDtypeStruct((share, table.shape[0], scores.shape[2]), jnp.float32),
        in_specs=[SMEM, VMEM],
        out_specs=VMEM,
        compiler_params=room((scores.shape, jnp.float32), ((8 * share, table.shape[0], scores.shape[2]), jnp.float32)),
        name="pick",
    )(table, *near(scores))


def body(activations, out_grads, proj_in, proj_out, queries, domains):
    seqs, length, width = activations.shape
    peers = lax.axis_size("dp")
    tensor_count = lax.axis_size("tensor")
    share = seqs // tensor_count
    swap = [(i, i ^ 1) for i in range(tensor_count)]
    meet = (peers // 2 + 1) % peers
    own = project(
        activations.reshape(seqs * length, width), out_grads.reshape(seqs * length, width), proj_in.T, proj_out.T
    )
    domains = domains.T
    other = lax.ppermute(own, "tensor", swap)
    table = plan(domains, own, share, peers, meet)
    kept, table = lax.optimization_barrier((queries, table))
    queries, own = lax.optimization_barrier((queries, own))
    other_queries = lax.ppermute(queries, "tensor", swap)
    queries = kept
    sent = spread(table, own, other, share, peers, tensor_count)
    groups = [
        [index * tensor_count + half_of(index, half, peers) for index in turned(peers, meet)]
        for half in range(tensor_count)
    ]
    came = lax.all_to_all(
        sent, ("dp", "tensor"), split_axis=0, concat_axis=0, tiled=True, axis_index_groups=groups
    )
    scores = score(came, queries, other_queries, meet)
    devices = peers * tensor_count
    back = lax.all_to_all(
        scores,
        ("dp", "tensor"),
        split_axis=0,
        concat_axis=0,
        tiled=True,
        axis_index_groups=[turned(devices, devices - 1)],
    )
    return pick(table, back, share, meet)


def solution(mesh):
    placed = (
        P(("groups", "dp"), None, "tensor"),
        P(("groups", "dp"), None, "tensor"),
        P("tensor", None),
        P("tensor", None),
        P(("groups", "dp", "tensor"), None),
        P(("groups", "dp"), None),
    )
    return jax.shard_map(
        body,
        mesh=mesh,
        in_specs=placed,
        out_specs=P(("groups", "dp", "tensor"), None, None),
        check_vma=False,
    )
```

```python
import functools
import math

import jax
import jax.numpy as jnp
from jax import lax
from jax.experimental import pallas as pl
from jax.experimental.pallas import tpu as pltpu
from jax.sharding import PartitionSpec as P

CAP = 2
LANES = 128
LAST = (((1,), (1,)), ((), ()))

VMEM = pl.BlockSpec(memory_space=pltpu.VMEM)
SMEM = pl.BlockSpec(memory_space=pltpu.SMEM)
ANY = pl.BlockSpec(memory_space=pl.ANY)


def half_of(index, core, peers):
    return core ^ (index >= 3 * peers // 4)


def my_half(peers):
    past = (lax.axis_index("dp") >= 3 * peers // 4).astype(jnp.int32)
    return lax.axis_index("tensor") ^ past


def turned(count, first):
    return [(first + i) % count for i in range(count)]


def each(count, step):
    if count <= 8:
        for at in range(count):
            step(at)
    else:
        lax.fori_loop(0, count, lambda at, _: (step(at), 0)[1], 0)


def near(*arrays):
    return [pltpu.with_memory_space_constraint(x, pltpu.VMEM) for x in arrays]


def far(*arrays):
    return [pltpu.with_memory_space_constraint(x, pltpu.HBM) for x in arrays]


def room(*shapes):
    held = sum(math.prod(shape) * jnp.dtype(dtype).itemsize for shape, dtype in shapes)
    return pltpu.CompilerParams(vmem_limit_bytes=2 * held + (1 << 20))


def project_kernel(acts, grads, p_in, p_out, out, x_v, w_v, sems):
    proj = p_in.shape[0]
    for side, (x, w) in enumerate(((grads, p_out), (acts, p_in))):
        pltpu.make_async_copy(x, x_v.at[side], sems.at[side, 1]).start()
        pltpu.make_async_copy(w, w_v.at[side, pl.ds(side * proj, proj)], sems.at[side, 0]).start()
    for side in range(2):
        w_v[side, pl.ds((1 - side) * proj, proj)] = jnp.zeros(p_in.shape, w_v.dtype)
    out[...] = jnp.zeros_like(out)

    @pl.loop(0, 2)
    def _(side):
        pltpu.make_async_copy(p_in, w_v.at[side, pl.ds(pl.multiple_of(side * proj, proj), proj)], sems.at[side, 0]).wait()
        pltpu.make_async_copy(acts, x_v.at[side], sems.at[side, 1]).wait()
        out[...] += lax.dot_general(x_v[side], w_v[side], LAST, preferred_element_type=jnp.float32)


def project(acts, grads, p_in, p_out):
    rows, width = acts.shape
    proj = p_in.shape[0]
    bf16 = jnp.bfloat16
    return pl.pallas_call(
        project_kernel,
        out_shape=jax.ShapeDtypeStruct((rows, 2 * proj), jnp.float32),
        in_specs=[ANY] * 4,
        out_specs=VMEM,
        scratch_shapes=[
            pltpu.VMEM((2, rows, width), bf16),
            pltpu.VMEM((2, 2 * proj, width), bf16),
            pltpu.SemaphoreType.DMA((2, 2)),
        ],
        compiler_params=room((acts.shape, bf16), ((4 * proj, width), bf16), ((rows, 2 * LANES), jnp.float32)),
        name="project",
    )(*far(acts, grads, p_in, p_out))


def rank(domains, row, first, named):
    fanout = domains.shape[0]
    found = jnp.int32(0)
    for other in range(first, row):
        if fanout <= 8:
            for k in range(fanout):
                found += (domains[k, other] == named).astype(jnp.int32)
        else:
            found = lax.fori_loop(
                0, fanout, lambda k, n, other=other: n + (domains[k, other] == named).astype(jnp.int32), found
            )
    return found


def feature_kernel(table, own, other, out, grams):
    fanout, seqs = table.shape
    length = own.shape[0] // seqs
    proj = own.shape[1] // 2
    half = out.shape[2]
    out[...] = jnp.zeros_like(out)
    both = own[...] + other[...]
    high = both.astype(jnp.bfloat16)
    low = (both - high.astype(jnp.float32)).astype(jnp.bfloat16)
    mine = my_half(out.shape[0]) * 2 * half
    left = lax.broadcasted_iota(jnp.int32, (half, LANES), 1) < proj
    for s in range(seqs):
        at = slice(s * length, (s + 1) * length)
        h, l = high[at], low[at]
        grams[s] = lax.dot_general(
            jnp.concatenate([h, l, h, l], axis=0)[:, :proj],
            jnp.concatenate([h, h, l, l], axis=0),
            (((0,), (0,)), ((), ())),
            preferred_element_type=jnp.float32,
        )
    for s in range(seqs):
        even = grams[s, pl.ds(mine, half, stride=2), :]
        odd = grams[s, pl.ds(mine + 1, half, stride=2), :]
        feature = jnp.where(left, pltpu.roll(even, proj, 1), odd).astype(out.dtype)

        def place(k, s=s, feature=feature):
            slot = table[k, s]
            out[slot // out.shape[1], slot % out.shape[1]] = feature

        each(fanout, place)


def spread(table, own, other, share, peers, tensor_count):
    seqs = table.shape[1]
    proj = own.shape[1] // 2
    half = proj * proj // LANES // tensor_count
    return pl.pallas_call(
        feature_kernel,
        out_shape=jax.ShapeDtypeStruct((peers, seqs // share * CAP, half, LANES), jnp.bfloat16),
        in_specs=[SMEM, VMEM, VMEM],
        out_specs=VMEM,
        scratch_shapes=[pltpu.VMEM((seqs, proj, 2 * proj), jnp.float32)],
        compiler_params=room(
            ((4 * own.shape[0], LANES), jnp.float32), ((peers, seqs // share * CAP, half, LANES), jnp.bfloat16)
        ),
        cost_estimate=pl.CostEstimate(flops=50_000_000_000, bytes_accessed=1 << 20, transcendentals=0),
        name="spread",
    )(table, *near(own, other))


def score_kernel(meet, features, own, other, out, rows_v):
    peers, slots, half, _ = features.shape
    count = peers * slots
    rows_v[...] = features[...].reshape(count * half, LANES).astype(jnp.float32)
    rows = jnp.concatenate(
        [rows_v[pl.ds(c, count, stride=half), :].astype(jnp.bfloat16) for c in range(half)], axis=1
    )
    me = lax.axis_index("tensor")
    part = pl.ds(pl.multiple_of(my_half(peers) * half * LANES, LANES), half * LANES)
    mine, theirs = (
        lax.dot_general(q[:, part], rows, LAST, preferred_element_type=jnp.float32)
        for q in (own, other)
    )
    scores = jnp.concatenate([jnp.where(me == 0, mine, theirs), jnp.where(me == 0, theirs, mine)], axis=0).T
    devices = out.shape[0]
    for p in range(devices):
        out[(p + devices // peers * meet + 1) % devices] = scores[p * CAP : (p + 1) * CAP]


def score(features, own, other, meet):
    peers, slots, half, _ = features.shape
    return pl.pallas_call(
        functools.partial(score_kernel, meet),
        out_shape=jax.ShapeDtypeStruct((peers * slots // CAP, CAP, 2 * own.shape[0]), jnp.float32),
        in_specs=[VMEM] * 3,
        out_specs=VMEM,
        scratch_shapes=[pltpu.VMEM((peers * slots * half, LANES), jnp.float32)],
        compiler_params=room(
            (features.shape, jnp.bfloat16),
            ((peers * slots * half, LANES), jnp.float32),
            ((2 * own.shape[0], own.shape[1]), jnp.bfloat16),
            ((peers * slots // CAP, 8, 2 * own.shape[0]), jnp.float32),
        ),
        name="score",
    )(*near(features, own, other))


def plan_kernel(share, peers, meet, domains, own, table):
    del own
    fanout, seqs = domains.shape
    groups = seqs // share
    for s in range(seqs):

        def place(k, s=s):
            named = domains[k, s]
            group = s // share
            owner = (named + peers - meet) % peers
            table[k, s] = (owner * groups + group) * CAP + rank(domains, s, group * share, named)

        each(fanout, place)


def plan(domains, own, share, peers, meet):
    return pl.pallas_call(
        functools.partial(plan_kernel, share, peers, meet),
        out_shape=pltpu.SMEM(domains.shape, jnp.int32),
        in_specs=[SMEM, ANY],
        out_specs=SMEM,
        compiler_params=room(),
        name="plan",
    )(domains, own)


def pick_kernel(meet, table, scores, out):
    share, fanout, _ = out.shape
    halves = table.shape[1] // share
    first = lax.axis_index("tensor") * share
    for s in range(share):

        def take(k, s=s):
            slot = table[k, first + s]
            at = (slot // (halves * CAP) + meet) * halves + 1
            both = scores[at % scores.shape[0]]
            for half in range(1, halves):
                both = both + scores[(at + half) % scores.shape[0]]
            out[s, pl.ds(k, 1)] = jnp.where(slot % CAP == 0, both[0:1], both[1:2])

        each(fanout, take)


def pick(table, scores, share, meet):
    return pl.pallas_call(
        functools.partial(pick_kernel, meet),
        out_shape=jax.ShapeDtypeStruct((share, table.shape[0], scores.shape[2]), jnp.float32),
        in_specs=[SMEM, VMEM],
        out_specs=VMEM,
        compiler_params=room((scores.shape, jnp.float32), ((8 * share, table.shape[0], scores.shape[2]), jnp.float32)),
        name="pick",
    )(table, *near(scores))


def body(activations, out_grads, proj_in, proj_out, queries, domains):
    seqs, length, width = activations.shape
    peers = lax.axis_size("dp")
    tensor_count = lax.axis_size("tensor")
    share = seqs // tensor_count
    swap = [(i, i ^ 1) for i in range(tensor_count)]
    meet = (peers // 2 + 1) % peers
    own = project(
        activations.reshape(seqs * length, width), out_grads.reshape(seqs * length, width), proj_in.T, proj_out.T
    )
    domains = domains.T
    other = lax.ppermute(own, "tensor", swap)
    table = plan(domains, own, share, peers, meet)
    kept, table = lax.optimization_barrier((queries, table))
    queries, own = lax.optimization_barrier((queries, own))
    other_queries = lax.ppermute(queries, "tensor", swap)
    queries = kept
    sent = spread(table, own, other, share, peers, tensor_count)
    groups = [
        [index * tensor_count + half_of(index, half, peers) for index in turned(peers, meet)]
        for half in range(tensor_count)
    ]
    came = lax.all_to_all(
        sent, ("dp", "tensor"), split_axis=0, concat_axis=0, tiled=True, axis_index_groups=groups
    )
    scores = score(came, queries, other_queries, meet)
    devices = peers * tensor_count
    back = lax.all_to_all(
        scores,
        ("dp", "tensor"),
        split_axis=0,
        concat_axis=0,
        tiled=True,
        axis_index_groups=[turned(devices, devices - 1)],
    )
    return pick(table, back, share, meet)


def solution(mesh):
    placed = (
        P(("groups", "dp"), None, "tensor"),
        P(("groups", "dp"), None, "tensor"),
        P("tensor", None),
        P("tensor", None),
        P(("groups", "dp", "tensor"), None),
        P(("groups", "dp"), None),
    )
    return jax.shard_map(
        body,
        mesh=mesh,
        in_specs=placed,
        out_specs=P(("groups", "dp", "tensor"), None, None),
        check_vma=False,
    )
```
